128 devices in a mesh: prow: 8 (over x, core), pcol: 16 (over y, z).
Axes of the slice: x: 4, y: 4, z: 4, core: 2. Of those that a mesh axis runs over, the one named last changes fastest.
Arguments:
- matrix: float32 [16384, 16384], P('prow', 'pcol'), may hold values from -1 to 14, as said below
Outputs:
- factor: float32 [16384, 16384], P('prow', 'pcol')
The draws below stay inside these ranges and needn't reach their ends.
Inputs may be any that keep to these rules, and one draw needn't show every extreme that they name: In natural order the matrix is symmetric positive definite.
All inputs are finite; a program needn't handle non-finite values.
Results may differ from the reference program's by a relative error of at most 0.0001.
Values sent between devices are 32-bit elements; how exact they have to be, the bound alone decides.
A program may use at most 128 MiB of HBM per device.

```python
import jax
import jax.numpy as jnp
from jax import lax

ORDER = 16384
NB = 256
STEPS = 4
N_PROW = 8
N_PCOL = 16


def draw_matrix(key, part):
    key = jax.random.fold_in(key, 11)
    keys = jax.random.split(key, 3)
    noise = jnp.clip(jax.random.normal(keys[0], (ORDER, ORDER), jnp.float32), -4.0, 4.0) * 0.1
    amplitude = 0.5
    reach = 0.3
    symmetric = (noise + noise.T) * 0.7071
    index = jnp.arange(ORDER)
    distance_blocks = jnp.abs(index[:, None] // NB - index[None, :] // NB).astype(jnp.float32)
    envelope = 1.0 / (1.0 + distance_blocks)
    samples = jax.random.uniform(keys[1], (ORDER, 4), jnp.float32)
    squared = jnp.zeros((ORDER, ORDER), jnp.float32)
    for feature in range(4):
        spread_now = samples[:, feature][:, None] - samples[:, feature][None, :]
        squared = squared + spread_now * spread_now
    kernel = amplitude * jnp.exp(-squared / (2.0 * reach * reach))
    nugget = 8.0 * (1.0 + 0.5 * jax.random.uniform(keys[2], (ORDER,), jnp.float32))
    full = jnp.where(index[:, None] == index[None, :], nugget[:, None] + amplitude, symmetric * envelope + kernel)
    row_blocks = ORDER // (NB * N_PROW)
    col_blocks = ORDER // (NB * N_PCOL)
    full = full.reshape(row_blocks, N_PROW, NB, ORDER).transpose(1, 0, 2, 3).reshape(ORDER, ORDER)
    full = full.reshape(ORDER, col_blocks, N_PCOL, NB).transpose(0, 2, 1, 3).reshape(ORDER, ORDER)
    return full


def setup_inputs(seed: int = 0) -> dict:
    seeds = jax.random.split(jax.random.key(seed), 2)
    matrix = draw_matrix(jax.random.fold_in(seeds[1], 71), 0)
    return {"matrix": matrix}


def natural_rows(stored, groups):
    blocks = ORDER // (NB * groups)
    return stored.reshape(groups, blocks, NB, ORDER).transpose(1, 0, 2, 3).reshape(ORDER, ORDER)

def natural_cols(stored, groups):
    blocks = ORDER // (NB * groups)
    return stored.reshape(ORDER, groups, blocks, NB).transpose(0, 2, 1, 3).reshape(ORDER, ORDER)

def storage_rows(natural, groups):
    blocks = ORDER // (NB * groups)
    return natural.reshape(blocks, groups, NB, ORDER).transpose(1, 0, 2, 3).reshape(ORDER, ORDER)

def storage_cols(natural, groups):
    blocks = ORDER // (NB * groups)
    return natural.reshape(ORDER, blocks, groups, NB).transpose(0, 2, 1, 3).reshape(ORDER, ORDER)

def reference(matrix):
    full = natural_cols(natural_rows(matrix, N_PROW), N_PCOL)
    for block in range(STEPS):
        first = block * NB
        last = first + NB
        triangle = jnp.linalg.cholesky(full[first:last, first:last])
        below = jax.scipy.linalg.solve_triangular(triangle, full[last:, first:last].T, lower=True).T
        trailing = full[last:, last:] - jnp.dot(below.astype(jnp.float32), below.T.astype(jnp.float32), precision=lax.Precision.HIGHEST, preferred_element_type=jnp.float32)
        full = full.at[last:, last:].set(trailing)
        column = jnp.concatenate([jnp.zeros((first, NB), jnp.float32), triangle, below], axis=0)
        full = full.at[:, first:last].set(column)
    return storage_cols(storage_rows(full, N_PROW), N_PCOL)
```

```python
import functools

import jax
import jax.numpy as jnp
from jax import lax
from jax.experimental import pallas as pl
from jax.experimental.pallas import tpu as pltpu
from jax.sharding import PartitionSpec as P

F32 = jnp.float32
BF16 = jnp.bfloat16
MESH = pl.DeviceIdType.MESH

TURNS = ((1, 0), (0, -1), (-1, 0), (0, 1))
PARENT = {
    (0, 1): 0, (1, 0): 2, (0, 3): 0, (3, 0): 2, (1, 1): 2, (1, 3): 2, (3, 3): 1, (3, 1): 3,
    (1, 2): 2, (2, 3): 1, (3, 2): 3, (2, 1): 2, (2, 2): 1, (2, 0): 2, (0, 2): 0,
}


def tree_tables():
    masks, depths = {}, {(0, 0): 0}
    for node in [(0, 0), *PARENT]:
        masks[node] = 0

    def depth(node):
        if node not in depths:
            dy, dz = TURNS[PARENT[node]]
            depths[node] = depth(((node[0] - dy) % 4, (node[1] - dz) % 4)) + 1
        return depths[node]

    for node, turn in PARENT.items():
        dy, dz = TURNS[turn]
        masks[(node[0] - dy) % 4, (node[1] - dz) % 4] |= 1 << turn
        depth(node)
    order = [(a, b) for a in range(4) for b in range(4)]
    return [masks[n] for n in order], [depths[n] for n in order]


MASKS, DEPTHS = tree_tables()
DEEPEST = max(DEPTHS)
LAG = 2
UNIT = 64
SLOTS = (((0, 0), (0, 1), (0, 2), (0, 3), (2, 2), (2, 3)), ((1, 1), (1, 2), (1, 3), (3, 3)))


def place():
    row, col = lax.axis_index("prow"), lax.axis_index("pcol")
    return row // 2, row % 2, col // 4, col % 4


def pick(index, values):
    out = jnp.int32(values[0])
    for i in range(1, len(values)):
        out = jnp.where(index == i, jnp.int32(values[i]), out)
    return out


def roles(y, z):
    table = []
    for s in range(4):
        a, b = y, (z - s + 4) % 4
        line = []
        for t in range(4):
            index = a * 4 + b
            mask, depth = pick(index, MASKS), pick(index, DEPTHS)
            flags = [None] * 4
            for d in range(4):
                flags[(d + t) % 4] = (mask // (1 << d)) % 2
            line.append((depth, flags))
            a, b = (4 - b) % 4, a
        table.append(line)
    return table


def comm_kernel(k_ref, ar_ref, z_ref, xs, xr, cs, cr, ks, kr, ps, pr, rs, rr, ls):
    x, core, y, z = place()
    mycol = y * 4 + z
    table = roles(y, z)

    def at(px, pcore, py, pz):
        return (px * 2 + pcore, py * 4 + pz)

    peer = at(x, 1 - core, y, z)
    others = [at((x + d) % 4, core, y, z) for d in (1, 2, 3)]
    around = [at(x, core, (y + dy + 4) % 4, (z + dz + 4) % 4) for dy, dz in TURNS]
    barrier = pltpu.get_barrier_semaphore()
    for device in [peer, *others, *around]:
        pl.semaphore_signal(barrier, inc=1, device_id=device, device_id_type=MESH)
    pl.semaphore_wait(barrier, 8)

    def remote(src, dst, ssem, rsem, device):
        return pltpu.make_async_remote_copy(src, dst, ssem, rsem, device_id=device, device_id_type=MESH)

    parts = ((0, 256), (256, 768))

    def top_rows(owner, part):
        first, width = parts[part]
        return z_ref.at[pl.ds(pl.multiple_of(owner * 256, 256), 256), pl.ds(1024 + first, width)]

    def own_top(part):
        first, width = parts[part]
        return k_ref.at[pl.ds(0, 256), pl.ds(first, width)]

    def x_copy(o, part, i):
        return remote(own_top(part), top_rows(o * 2 + core, part), xs.at[part, i], xr.at[o, part], others[i])

    def x_keep(o, part):
        return pltpu.make_async_copy(own_top(part), top_rows(o * 2 + core, part), ls.at[part])

    def peer_first(o, part):
        return remote(own_top(part), top_rows(o * 2 + core, part), cs.at[o, part], cr.at[o, part], peer)

    def peer_next(o, part, owner_core):
        block = top_rows(o * 2 + owner_core, part)
        return remote(block, block, cs.at[o, part], cr.at[o, part], peer)

    for part in range(2):
        for o in range(2):

            @pl.when(x == o)
            def _():
                for i in range(3):
                    x_copy(o, part, i).start()
                peer_first(o, part).start()
                x_keep(o, part).start()

    keep_column = pltpu.make_async_copy(
        k_ref.at[:, pl.ds(0, 256)], ar_ref.at[:, pl.ds(pl.multiple_of(z * 256, 256), 256)], ls.at[2]
    )

    @pl.when(y == 0)
    def _():
        keep_column.start()

    def x_arrive(part):
        for o in range(2):

            @pl.when(x != o)
            def _():
                x_copy(o, part, 0).wait_recv()
                peer_next(o, part, core).start()

            @pl.when(x == o)
            def _():
                x_keep(o, part).wait()

    def peer_arrive(part):
        for o in range(2):
            peer_next(o, part, 1 - core).wait_recv()

    x_arrive(0)

    def slot(i, own):
        first, second = SLOTS if own else SLOTS[::-1]
        if i < len(SLOTS[1]):
            pair = lambda u: jnp.where(core == 0, first[i][u], second[i][u])
            return pair(0), pair(1), None
        full = max(SLOTS, key=len)[i]
        return jnp.int32(full[0]), jnp.int32(full[1]), (core == 0) if own else (core == 1)

    def lead(b, s, t, width=UNIT):
        return z_ref.at[pl.ds(pl.multiple_of(b * 256 + t * UNIT, UNIT), width), pl.ds(pl.multiple_of(s * 256, 256), 256)]

    def lead_own(b, t):
        return z_ref.at[pl.ds(pl.multiple_of(b * 256 + t * UNIT, UNIT), UNIT), pl.ds(1024, 256)]

    def role(s, t):
        depth = table[3][t][0]
        flags = list(table[3][t][1])
        for o in range(3):
            depth = jnp.where(s == o, table[o][t][0], depth)
            flags = [jnp.where(s == o, a, b) for a, b in zip(table[o][t][1], flags)]
        return depth, flags

    lead_roles = []
    for i in range(6):
        b, s, used = slot(i, True)
        lead_roles.append([role(s, t) for t in range(4)])

    def lead_tick(tick):
        for i in range(6):
            b, s, used = slot(i, True)
            for t in range(4):
                depth, flags = lead_roles[i][t]
                now = tick == i + LAG * depth
                if used is not None:
                    now = now & used
                block = lead(b, s, t)

                @pl.when(now & (depth == 0))
                def _():
                    for d in range(4):

                        @pl.when(flags[d] == 1)
                        def _():
                            remote(lead_own(b, t), block, ks.at[i, t, d], kr.at[i, t], around[d]).start()

                @pl.when(now & (depth != 0))
                def _():
                    remote(block, block, ks.at[i, t, 0], kr.at[i, t], peer).wait_recv()
                    for d in range(4):

                        @pl.when(flags[d] == 1)
                        def _():
                            remote(block, block, ks.at[i, t, d], kr.at[i, t], around[d]).start()

                    remote(block, block, ps.at[i, t], pr.at[i, t], peer).start()

    def lead_finish_sends():
        for i in range(6):
            b, s, used = slot(i, True)
            for t in range(4):
                depth, flags = lead_roles[i][t]
                block = lead(b, s, t)
                ok = jnp.bool_(True) if used is None else used
                for d in range(4):

                    @pl.when(ok & (flags[d] == 1))
                    def _():
                        remote(block, block, ks.at[i, t, d], kr.at[i, t], around[d]).wait_send()

                @pl.when(ok & (depth != 0))
                def _():
                    remote(block, block, ps.at[i, t], pr.at[i, t], peer).wait_send()

    def lead_arrive():
        for i in range(6):
            b, s, used = slot(i, False)
            ok = mycol != s
            if used is not None:
                ok = ok & used
            for t in range(4):
                block = lead(b, s, t)

                @pl.when(ok)
                def _():
                    remote(block, block, ps.at[i, t], pr.at[i, t], peer).wait_recv()

    def unit(s, t, q):
        return pl.ds(pl.multiple_of(t * 512 + q * UNIT, UNIT), UNIT), pl.ds(s * 256, 256)

    def row_tick(tick):
        for s in range(4):
            for t in range(4):
                depth, flags = table[s][t]
                q = tick - (6 + 8 * s) - LAG * depth
                now = (q >= 0) & (q < 8)
                rows, cols = unit(s, t, q)

                @pl.when(now & (depth == 0))
                def _():
                    for d in range(4):

                        @pl.when(flags[d] == 1)
                        def _():
                            remote(
                                k_ref.at[rows, pl.ds(0, 256)], ar_ref.at[rows, cols], rs.at[s, t, d], rr.at[s, t, q], around[d]
                            ).start()

                @pl.when(now & (depth != 0))
                def _():
                    block = ar_ref.at[rows, cols]
                    remote(block, block, rs.at[s, t, 0], rr.at[s, t, q], peer).wait_recv()
                    for d in range(4):

                        @pl.when(flags[d] == 1)
                        def _():
                            remote(block, block, rs.at[s, t, d], rr.at[s, t, q], around[d]).start()

    def row_finish_sends():
        for s in range(4):
            for t in range(4):
                depth, flags = table[s][t]
                block = ar_ref.at[pl.ds(t * 512, 512), pl.ds(s * 256, 256)]
                for d in range(4):

                    @pl.when(flags[d] == 1)
                    def _():
                        remote(block, block, rs.at[s, t, d], rr.at[s, t, 0], around[d]).wait_send()

    lead_ticks = 6 + LAG * DEEPEST
    row_ticks = 6 + 32 + LAG * DEEPEST

    @pl.loop(0, lead_ticks)
    def _(tick):
        lead_tick(tick)
        row_tick(tick)

    peer_arrive(0)

    @pl.when(y == 0)
    def _():
        pltpu.make_async_copy(z_ref.at[:, pl.ds(1024, 256)], z_ref.at[:, pl.ds(pl.multiple_of(z * 256, 256), 256)], ls.at[0]).start()

    x_arrive(1)
    lead_arrive()

    @pl.loop(lead_ticks, row_ticks)
    def _(tick):
        row_tick(tick)

    @pl.when(y == 0)
    def _():
        keep_column.wait()
        pltpu.make_async_copy(z_ref.at[:, pl.ds(1024, 256)], z_ref.at[:, pl.ds(pl.multiple_of(z * 256, 256), 256)], ls.at[0]).wait()

    peer_arrive(1)
    for part in range(2):
        for o in range(2):

            @pl.when(x == o)
            def _():
                for i in range(3):
                    x_copy(o, part, i).wait_send()
                peer_first(o, part).wait_send()

            @pl.when(x != o)
            def _():
                peer_next(o, part, core).wait_send()

    lead_finish_sends()
    row_finish_sends()


def gather(matrix):
    sems = [(2, 3), (2, 2), (2, 2), (2, 2), (6, 4, 4), (6, 4), (6, 4), (6, 4), (4, 4, 4), (4, 4, 8), (3,)]
    return pl.pallas_call(
        comm_kernel,
        out_shape=[jax.ShapeDtypeStruct((2048, 1024), F32), jax.ShapeDtypeStruct((1024, 2048), F32)],
        in_specs=[pl.BlockSpec(memory_space=pl.ANY)],
        out_specs=[pl.BlockSpec(memory_space=pl.ANY)] * 2,
        scratch_shapes=[pltpu.SemaphoreType.DMA(s) for s in sems],
        compiler_params=pltpu.CompilerParams(collective_id=0, has_side_effects=True),
        name="gather",
    )(matrix)


def split(a):
    high = a.astype(BF16)
    return high, (a - high.astype(F32)).astype(BF16)


def product(a, b):
    dot = functools.partial(jnp.dot, preferred_element_type=F32)
    return dot(a[0], b[0]) + (dot(a[0], b[1]) + dot(a[1], b[0]))


def lanes(block, j):
    return jnp.take_along_axis(block, jnp.full((8, 128), j, jnp.int32), axis=1)


def rows_of(block, i):
    return jnp.broadcast_to(block[i : i + 1], (8, 128))


def triangle128(load, upper_ref, inverse_ref):
    lane = lax.broadcasted_iota(jnp.int32, (8, 128), 1)
    sub = lax.broadcasted_iota(jnp.int32, (8, 128), 0)
    strips = [load(v) for v in range(16)]
    for b in range(16):
        first, count = 8 * b, 16 - b
        inside = (lane >= first) & (lane < first + 8)
        columns = [lanes(strips[b], first + i) for i in range(8)]
        pivot = [[rows_of(columns[i], k) for k in range(8)] for i in range(8)]
        start = jnp.where(inside, jnp.where(lane == sub + first, 1.0, 0.0), strips[b])
        rows = [rows_of(start, i) for i in range(8)]
        if count > 1:
            below = [lanes(strips[b + 1], first + i) for i in range(8)]
            after = jnp.where(inside, 0.0, strips[b + 1])
        scales, factors = [], []
        for i in range(8):
            scale = 1.0 / pivot[i][i]
            scales.append(scale)
            factor = [None] * 8
            for j in range(i + 1, 8):
                factor[j] = pivot[i][j] * scale
            factors.append(factor)
            for j in range(i + 1, 8):
                pivot[j][j] = pivot[j][j] - (pivot[i][j] * pivot[i][j]) * scale
                for k in range(j + 1, 8):
                    pivot[j][k] = pivot[j][k] - factor[j] * pivot[i][k]
                rows[j] = rows[j] - factor[j] * rows[i]
            if count > 1:
                weight = below[i] * scale
                for k in range(i + 1, 8):
                    below[k] = below[k] - weight * pivot[i][k]
                after = after - weight * rows[i]
        if count > 2:
            solved = [None] * 8
            for i in range(7, -1, -1):
                row = rows[i] * scales[i]
                for k in range(i + 1, 8):
                    row = row - factors[i][k] * solved[k]
                solved[i] = row
            for v in range(2, count):
                strip = jnp.where(inside, 0.0, strips[b + v])
                for i in range(8):
                    strip = strip - lanes(strips[b + v], first + i) * solved[i]
                strips[b + v] = strip
        if count > 1:
            strips[b + 1] = after
        inverse = upper = None
        for i in range(7, -1, -1):
            root = lax.rsqrt(pivot[i][i])
            left = rows[i] * root
            right = left
            for k in range(i, 8):
                right = jnp.where(lane == first + k, pivot[i][k] * root, right)
            inverse = left if inverse is None else jnp.where(sub == i, left, inverse)
            upper = right if upper is None else jnp.where(sub == i, right, upper)
        upper_ref[first : first + 8, :] = jnp.where(lane >= sub + first, upper, 0.0)
        inverse_ref[first : first + 8, :] = jnp.where(lane <= sub + first, inverse, 0.0)


TILE = 512


def factor_kernel(z_ref, wh_ref, wl_ref, top_ref, z, inverse, upper, ph, pw):
    row, col = lax.axis_index("prow"), lax.axis_index("pcol")
    z[...] = z_ref[...]

    @pl.loop(0, 4)
    def _(step):
        o = pl.multiple_of(step * 256, 256)

        @pl.when(row == step)
        def _():
            top_ref[...] = z[pl.ds(o, 256), 1024:2048]

        for half in range(2):
            at = pl.multiple_of(o + 128 * half, 128)
            diagonal = (pl.ds(at, 128), pl.ds(at, 128))
            triangle128(
                lambda v: z[pl.ds(pl.multiple_of(at + 8 * v, 8), 8), pl.ds(at, 128)],
                upper,
                inverse.at[step * 2 + half],
            )
            scale = split(inverse[step * 2 + half])

            @pl.loop(0, 2048, step=TILE)
            def _(c):
                cols = pl.ds(pl.multiple_of(c, TILE), TILE)
                z[pl.ds(at, 128), cols] = product(scale, split(z[pl.ds(at, 128), cols]))

            z[diagonal] = upper[...]
            if half == 0:
                next_at = pl.multiple_of(o + 128, 128)
                side = split(z[pl.ds(at, 128), pl.ds(next_at, 128)].T)

                @pl.loop(0, 2048, step=TILE)
                def _(c):
                    cols = pl.ds(pl.multiple_of(c, TILE), TILE)
                    z[pl.ds(next_at, 128), cols] -= product(side, split(z[pl.ds(at, 128), cols]))

            else:
                z[pl.ds(at, 128), pl.ds(o, 128)] = jnp.zeros((128, 128), F32)

        @pl.loop(0, 2048, step=TILE)
        def _(c):
            cols = pl.ds(pl.multiple_of(c, TILE), TILE)
            ph[:, cols], pw[:, cols] = split(z[pl.ds(o, 256), cols])

        @pl.loop(step + 1, 4)
        def _(i):
            at = pl.multiple_of(i * 256, 256)
            side = split(z[pl.ds(o, 256), pl.ds(at, 256)].T)

            @pl.loop(0, 2048, step=TILE)
            def _(c):
                cols = pl.ds(pl.multiple_of(c, TILE), TILE)
                z[pl.ds(at, 256), cols] -= product(side, (ph[:, cols], pw[:, cols]))

    @pl.when((col < 4) & (row < 4) & (row >= col))
    def _():
        block = z[pl.ds(pl.multiple_of(jnp.minimum(col, 3) * 256, 256), 256), pl.ds(pl.multiple_of(jnp.minimum(row, 3) * 256, 256), 256)]
        top_ref[:, 0:256] = block.T

    @pl.when((col < 4) & (row < col))
    def _():
        top_ref[:, 0:256] = jnp.zeros((256, 256), F32)

    @pl.when(col < 4)
    def _():
        a = lax.broadcasted_iota(jnp.int32, (1024, 256), 0)
        b = lax.broadcasted_iota(jnp.int32, (1024, 256), 1)
        z[:, 1024:1280] = jnp.where(a == b + col * 256, -1.0, 0.0)

    for step in range(3, -1, -1):
        o = 256 * step
        side = split(z[o : o + 256, o + 256 : 1024]) if step < 3 else None
        first = split(inverse[2 * step].T)
        second = split(inverse[2 * step + 1].T)
        between = split(z[o : o + 128, o + 128 : o + 256])

        @pl.loop(0, 1024, step=TILE)
        def _(c):
            cols = pl.ds(pl.multiple_of(c, TILE), TILE)
            mine = z[o : o + 256, pl.ds(pl.multiple_of(c + 1024, TILE), TILE)]
            if step < 3:
                mine = mine - product(side, (wh_ref[o + 256 : 1024, cols], wl_ref[o + 256 : 1024, cols]))
            low = split(product(second, split(mine[128:])))
            wh_ref[o + 128 : o + 256, cols], wl_ref[o + 128 : o + 256, cols] = low
            high = split(product(first, split(mine[:128] - product(between, low))))
            wh_ref[o : o + 128, cols], wl_ref[o : o + 128, cols] = high


def weights(z):
    return pl.pallas_call(
        factor_kernel,
        out_shape=[
            jax.ShapeDtypeStruct((1024, 1024), BF16),
            jax.ShapeDtypeStruct((1024, 1024), BF16),
            jax.ShapeDtypeStruct((256, 1024), F32),
        ],
        scratch_shapes=[
            pltpu.VMEM((1024, 2048), F32),
            pltpu.VMEM((8, 128, 128), F32),
            pltpu.VMEM((128, 128), F32),
            pltpu.VMEM((256, 2048), BF16),
            pltpu.VMEM((256, 2048), BF16),
        ],
        compiler_params=pltpu.CompilerParams(vmem_limit_bytes=52 << 20),
        name="weights",
    )(z)


def update_kernel(m_ref, a_ref, wh_ref, wl_ref, top_ref, out_ref):
    row, col = lax.axis_index("prow"), lax.axis_index("pcol")
    out_ref[...] = m_ref[...]

    @pl.when(col < 4)
    def _():
        out_ref[:, 0:256] = jnp.zeros((256, 256), F32)

    out_ref[...] -= product(split(a_ref[...]), (wh_ref[...], wl_ref[...]))

    @pl.when((pl.program_id(0) == 0) & (row < 4))
    def _():
        out_ref[...] = top_ref[...]


def update(matrix, column, wh, wl, top):
    tile = pl.BlockSpec((256, 1024), lambda i: (i, 0))
    whole = lambda shape: pl.BlockSpec(shape, lambda i: (0, 0))
    return pl.pallas_call(
        update_kernel,
        grid=(8,),
        out_shape=jax.ShapeDtypeStruct((2048, 1024), F32),
        in_specs=[tile, tile, whole((1024, 1024)), whole((1024, 1024)), whole((256, 1024))],
        out_specs=tile,
        compiler_params=pltpu.CompilerParams(vmem_limit_bytes=48 << 20),
        name="update",
    )(matrix, column, wh, wl, top)


def shards(matrix):
    column, z = gather(matrix)
    wh, wl, top = weights(z)
    return update(matrix, column, wh, wl, top)


def solution(mesh):
    return jax.shard_map(
        shards,
        mesh=mesh,
        in_specs=(P("prow", "pcol"),),
        out_specs=P("prow", "pcol"),
        check_vma=False,
    )
```

```python
import functools

import jax
import jax.numpy as jnp
from jax import lax
from jax.experimental import pallas as pl
from jax.experimental.pallas import tpu as pltpu
from jax.sharding import PartitionSpec as P

F32 = jnp.float32
BF16 = jnp.bfloat16
MESH = pl.DeviceIdType.MESH

TURNS = ((1, 0), (0, -1), (-1, 0), (0, 1))
PARENT = {
    (0, 1): 0, (1, 0): 2, (0, 3): 0, (3, 0): 2, (1, 1): 2, (1, 3): 2, (3, 3): 1, (3, 1): 3,
    (1, 2): 2, (2, 3): 1, (3, 2): 3, (2, 1): 2, (2, 2): 1, (2, 0): 2, (0, 2): 0,
}


def tree_children():
    trees = []
    parent = dict(PARENT)
    for _ in range(4):
        children = {(a, b): [] for a in range(4) for b in range(4)}
        for node, turn in parent.items():
            dy, dz = TURNS[turn]
            children[(node[0] - dy) % 4, (node[1] - dz) % 4].append(turn)
        trees.append(children)
        parent = {(n[1] % 4, -n[0] % 4): (d + 1) % 4 for n, d in parent.items()}
    return trees


CHILDREN = tree_children()
UNIT = 64
LEAD = 2

PREFIX = 48
ORDER = (
    (
        8, 72, 136, 200, 73, 203, 74, 202, 0, 64, 128, 192, 4, 68, 132, 196, 201, 75, 9, 137,
        11, 139, 65, 195, 69, 199, 10, 138, 66, 194, 70, 198, 193, 67, 129, 131, 1, 3, 197, 71,
        5, 133, 7, 135, 130, 2, 6, 134, 12, 76, 140, 204, 16, 80, 144, 208, 20, 84, 148, 212,
        24, 88, 152, 216, 28, 92, 156, 220, 32, 96, 160, 224, 36, 100, 164, 228, 77, 207, 81, 211,
        85, 215, 89, 219, 93, 223, 13, 141, 15, 143, 97, 227, 101, 231, 17, 145, 19, 147, 78, 206,
        82, 210, 149, 23, 21, 151, 86, 214, 14, 90, 218, 142, 153, 27, 94, 222, 25, 98, 226, 155,
        157, 31, 102, 230, 18, 205, 79, 146, 161, 35, 209, 83, 29, 159, 213, 87, 165, 39, 217, 91,
        22, 150, 33, 163, 221, 95, 225, 99, 229, 103, 26, 154, 37, 167, 30, 158, 34, 162, 38, 166,
    ),
    (
        136, 137, 139, 73, 203, 8, 202, 72, 200, 74, 138, 128, 132, 201, 9, 11, 75, 129, 131, 65,
        195, 133, 135, 69, 10, 199, 64, 66, 194, 0, 192, 130, 4, 198, 68, 70, 196, 134, 193, 1,
        3, 67, 197, 71, 5, 7, 2, 6, 140, 144, 148, 141, 143, 152, 145, 147, 156, 149, 12, 151,
        160, 142, 153, 16, 164, 155, 157, 20, 146, 161, 15, 77, 207, 159, 165, 13, 19, 150, 81, 211,
        163, 78, 24, 204, 85, 215, 167, 208, 82, 154, 14, 17, 23, 76, 79, 89, 219, 158, 28, 212,
        86, 80, 93, 223, 83, 162, 18, 21, 27, 84, 32, 97, 227, 216, 90, 166, 88, 231, 22, 101,
        87, 92, 220, 94, 206, 96, 31, 36, 25, 210, 100, 205, 224, 98, 214, 26, 91, 35, 218, 209,
        222, 213, 228, 102, 29, 226, 217, 95, 39, 30, 230, 221, 33, 99, 225, 229, 34, 103, 37, 38,
    ),
    (
        8, 136, 137, 11, 9, 73, 139, 203, 74, 202, 72, 200, 10, 138, 0, 128, 4, 132, 201, 75,
        129, 3, 1, 65, 131, 195, 133, 7, 5, 69, 135, 199, 194, 130, 66, 64, 2, 192, 198, 70,
        68, 196, 6, 134, 67, 193, 71, 197, 12, 140, 16, 144, 15, 141, 20, 148, 13, 143, 19, 145,
        24, 152, 149, 23, 14, 142, 17, 147, 28, 156, 18, 146, 27, 153, 21, 151, 32, 160, 22, 150,
        31, 157, 36, 164, 25, 155, 26, 154, 35, 161, 207, 77, 29, 159, 39, 165, 211, 81, 30, 158,
        33, 163, 76, 204, 34, 162, 215, 85, 37, 167, 219, 89, 80, 38, 208, 166, 223, 93, 84, 212,
        227, 97, 88, 216, 92, 220, 231, 101, 78, 206, 96, 224, 82, 210, 100, 228, 205, 79, 86, 214,
        90, 218, 209, 83, 94, 222, 213, 87, 98, 226, 217, 91, 102, 230, 221, 95, 225, 99, 229, 103,
    ),
    (
        8, 9, 11, 73, 203, 136, 74, 72, 200, 10, 202, 0, 4, 75, 137, 139, 1, 3, 201, 65,
        195, 5, 7, 69, 138, 199, 64, 2, 128, 66, 192, 194, 132, 70, 68, 6, 196, 198, 129, 67,
        193, 131, 71, 133, 197, 135, 130, 134, 12, 16, 20, 13, 15, 24, 17, 19, 28, 23, 140, 21,
        32, 14, 27, 144, 36, 25, 31, 148, 18, 35, 141, 77, 207, 29, 39, 143, 145, 22, 81, 211,
        33, 206, 152, 76, 85, 215, 37, 80, 210, 26, 142, 147, 149, 204, 205, 89, 219, 30, 156, 84,
        214, 208, 93, 223, 209, 34, 146, 151, 153, 212, 160, 97, 227, 88, 218, 38, 216, 101, 150, 231,
        213, 92, 220, 222, 78, 224, 157, 164, 155, 82, 228, 79, 96, 226, 86, 154, 217, 161, 90, 83,
        94, 87, 100, 230, 159, 98, 91, 221, 165, 158, 102, 95, 163, 225, 99, 103, 162, 229, 167, 166,
    ),
)


def place():
    row, col = lax.axis_index("prow"), lax.axis_index("pcol")
    return row // 2, row % 2, col // 4, col % 4


def pick(index, values):
    out = jnp.int32(values[0])
    for i in range(1, len(values)):
        if values[i] != values[0] or len(set(values)) > 1:
            out = jnp.where(index == i, jnp.int32(values[i]), out)
    return out


def packed(y, code):
    dz, tree = code % 4, code // 64
    links = sum(1 << d for d in CHILDREN[tree][y, dz])
    return code + 256 * ((y == 0 and dz == 0) + 2 * links)


def split(a):
    high = a.astype(BF16)
    return high, (a - high.astype(F32)).astype(BF16)


def product(a, b):
    dot = functools.partial(jnp.dot, preferred_element_type=F32)
    return dot(a[0], b[0]) + (dot(a[0], b[1]) + dot(a[1], b[0]))


def lanes(block, j):
    return jnp.take_along_axis(block, jnp.full((8, 128), j, jnp.int32), axis=1)


def rows_of(block, i):
    return jnp.broadcast_to(block[i : i + 1], (8, 128))


def triangle128(load, upper_ref, inverse_ref, hook):
    lane = lax.broadcasted_iota(jnp.int32, (8, 128), 1)
    sub = lax.broadcasted_iota(jnp.int32, (8, 128), 0)
    strips = [load(v) for v in range(16)]
    for b in range(16):
        first, count = 8 * b, 16 - b
        inside = (lane >= first) & (lane < first + 8)
        columns = [lanes(strips[b], first + i) for i in range(8)]
        pivot = [[rows_of(columns[i], k) for k in range(8)] for i in range(8)]
        start = jnp.where(inside, jnp.where(lane == sub + first, 1.0, 0.0), strips[b])
        rows = [rows_of(start, i) for i in range(8)]
        if count > 1:
            below = [lanes(strips[b + 1], first + i) for i in range(8)]
            after = jnp.where(inside, 0.0, strips[b + 1])
        scales, factors = [], []
        for i in range(8):
            scale = 1.0 / pivot[i][i]
            scales.append(scale)
            factor = [None] * 8
            for j in range(i + 1, 8):
                factor[j] = pivot[i][j] * scale
            factors.append(factor)
            for j in range(i + 1, 8):
                pivot[j][j] = pivot[j][j] - (pivot[i][j] * pivot[i][j]) * scale
                for k in range(j + 1, 8):
                    pivot[j][k] = pivot[j][k] - factor[j] * pivot[i][k]
                rows[j] = rows[j] - factor[j] * rows[i]
            if count > 1:
                weight = below[i] * scale
                for k in range(i + 1, 8):
                    below[k] = below[k] - weight * pivot[i][k]
                after = after - weight * rows[i]
        if count > 2:
            solved = [None] * 8
            for i in range(7, -1, -1):
                row = rows[i] * scales[i]
                for k in range(i + 1, 8):
                    row = row - factors[i][k] * solved[k]
                solved[i] = row
            for v in range(2, count):
                strip = jnp.where(inside, 0.0, strips[b + v])
                for i in range(8):
                    strip = strip - lanes(strips[b + v], first + i) * solved[i]
                strips[b + v] = strip
        if count > 1:
            strips[b + 1] = after
        hook(b)
        inverse = upper = None
        for i in range(7, -1, -1):
            root = lax.rsqrt(pivot[i][i])
            left = rows[i] * root
            right = left
            for k in range(i, 8):
                right = jnp.where(lane == first + k, pivot[i][k] * root, right)
            inverse = left if inverse is None else jnp.where(sub == i, left, inverse)
            upper = right if upper is None else jnp.where(sub == i, right, upper)
        upper_ref[first : first + 8, :] = jnp.where(lane >= sub + first, upper, 0.0)
        inverse_ref[first : first + 8, :] = jnp.where(lane <= sub + first, inverse, 0.0)


TILE = 512


def panels_kernel(
    k_ref, ar_out, wh_ref, wl_ref, top_ref, ar, z, inverse, upper, inverse_high, inverse_low, order, xs, xr, cs, cr, ks, kr, ps, pr, rs, rr, ls
):
    x, core, y, zz = place()
    row, col = x * 2 + core, y * 4 + zz

    def at(px, pcore, py, pz):
        return (px * 2 + pcore, py * 4 + pz)

    peer = at(x, 1 - core, y, zz)
    after, before = at((x + 1) % 4, core, y, zz), at((x + 3) % 4, core, y, zz)
    around = [at(x, core, (y + dy + 4) % 4, (zz + dz + 4) % 4) for dy, dz in TURNS]
    barrier = pltpu.get_barrier_semaphore()
    for device in [peer, after, before, *around]:
        pl.semaphore_signal(barrier, inc=1, device_id=device, device_id_type=MESH)

    keep_column = pltpu.make_async_copy(k_ref.at[:, pl.ds(0, 256)], ar.at[zz], ls.at[4])

    @pl.when(y == 0)
    def _():
        keep_column.start()

    for e in range(16 * (LEAD + 8)):
        order[e] = pick(y, [packed(i, ORDER[i][e]) for i in range(4)])

    pl.semaphore_wait(barrier, 7)

    def remote(src, dst, ssem, rsem, device):
        return pltpu.make_async_remote_copy(src, dst, ssem, rsem, device_id=device, device_id_type=MESH)

    def top_rows(o, of_core, part):
        return z.at[pl.ds(pl.multiple_of(o * 512 + of_core * 256, 256), 256), pl.ds(1024 + 256 * part, 256)]

    def own_top(part):
        return k_ref.at[pl.ds(0, 256), pl.ds(256 * part, 256)]

    def x_own(o, part, i):
        return remote(own_top(part), top_rows(o, core, part), xs.at[part, i], xr.at[o, part], (after, before)[i])

    def x_pass(o, part, device):
        block = top_rows(o, core, part)
        return remote(block, block, xs.at[part, 0], xr.at[o, part], device)

    def x_keep(o, part):
        return pltpu.make_async_copy(own_top(part), top_rows(o, core, part), ls.at[part])

    def peer_own(o, part):
        return remote(own_top(part), top_rows(o, core, part), cs.at[o, part], cr.at[o, part], peer)

    def peer_pass(o, part, of_core):
        block = top_rows(o, of_core, part)
        return remote(block, block, cs.at[o, part], cr.at[o, part], peer)

    def x_start(part):
        for o in range(2):

            @pl.when(x == o)
            def _():
                x_own(o, part, 0).start()
                x_own(o, part, 1).start()
                peer_own(o, part).start()
                x_keep(o, part).start()

    def x_near(part):
        for o in range(2):

            @pl.when(x == 1 - o)
            def _():
                x_pass(o, part, peer).wait_recv()
                peer_pass(o, part, core).start()
                x_keep(1 - o, part).wait()

        for near, mine, device in ((1, 2, after), (0, 3, before)):

            @pl.when(x == mine)
            def _():
                x_pass(near, part, device).wait_recv()
                x_pass(near, part, device).start()
                peer_pass(near, part, core).start()

    def x_far(part):
        for far, mine in ((0, 2), (1, 3)):

            @pl.when(x == mine)
            def _():
                x_pass(far, part, peer).wait_recv()
                peer_pass(far, part, core).start()

    def peer_take(part):
        for o in range(2):
            peer_pass(o, part, 1 - core).wait_recv()

    def x_finish():
        for part in range(4):
            for o in range(2):

                @pl.when(x == o)
                def _():
                    x_own(o, part, 0).wait_send()
                    x_own(o, part, 1).wait_send()
                    peer_own(o, part).wait_send()
                    peer_pass(1 - o, part, core).wait_send()

            @pl.when(x >= 2)
            def _():
                x_pass(0, part, peer).wait_send()
                for o in range(2):
                    peer_pass(o, part, core).wait_send()

    def lead_block(s, unit, of_core):
        start = pl.multiple_of((unit // 2) * 256 + of_core * 128 + (unit % 2) * UNIT, UNIT)
        return z.at[pl.ds(start, UNIT), pl.ds(pl.multiple_of(s * 256, 256), 256)]

    def lead_root(unit):
        start = pl.multiple_of((unit // 2) * 256 + core * 128 + (unit % 2) * UNIT, UNIT)
        return z.at[pl.ds(start, UNIT), pl.ds(1024, 256)]

    def row_block(s, t, q):
        return ar.at[s, pl.ds(pl.multiple_of(t * 512 + q * UNIT, UNIT), UNIT)]

    def forward(e, leading):
        code = order[e]
        s = (zz - code % 4 + 4) % 4
        q = (code // 4) % 16
        t = (code // 64) % 4
        root = (code // 256) % 2
        links = code // 512
        flags = [(links // (1 << d)) % 2 == 1 for d in range(4)]
        if leading:
            unit = q * 4 + t
            lead = (q < LEAD) & (unit // 2 <= s)

            @pl.when(lead & (root == 1))
            def _():
                for d in range(4):

                    @pl.when(flags[d])
                    def _():
                        remote(lead_root(unit), lead_block(s, unit, core), ks.at[s, unit, d], kr.at[s, unit], around[d]).start()

            @pl.when(lead & (root == 0))
            def _():
                block = lead_block(s, unit, core)
                remote(block, block, ps.at[s, unit], kr.at[s, unit], peer).wait_recv()
                for d in range(4):

                    @pl.when(flags[d])
                    def _():
                        remote(block, block, ks.at[s, unit, d], kr.at[s, unit], around[d]).start()

                remote(block, block, ps.at[s, unit], pr.at[s, unit], peer).start()

        def pass_row():
            n = q - LEAD
            block = row_block(s, t, n)

            @pl.when(root == 0)
            def _():
                remote(block, block, rs.at[s, t, 0], rr.at[s, t, n], peer).wait_recv()

            for d in range(4):

                @pl.when(flags[d] & ((root == 0) | (n > 0)))
                def _():
                    remote(block, block, rs.at[s, t, d], rr.at[s, t, n], around[d]).start()

        if leading:
            pl.when(q >= LEAD)(pass_row)
        else:
            pass_row()

    x_start(0)

    @pl.when(y == 0)
    def _():
        keep_column.wait()
        for t in range(4):
            (d,) = CHILDREN[t][0, 0]
            block = row_block(zz, t, 0)
            remote(block, block, rs.at[zz, t, d], rr.at[zz, t, 0], around[d]).start()

    x_near(0)
    x_far(0)
    peer_take(0)
    keep_lead = pltpu.make_async_copy(z.at[:, pl.ds(1024, 256)], z.at[:, pl.ds(pl.multiple_of(zz * 256, 256), 256)], ls.at[5])

    @pl.when(y == 0)
    def _():
        keep_lead.start()

    for part in range(1, 4):
        x_start(part)

    for part in range(1, 4):

        @pl.loop((part - 1) * (PREFIX // 3), part * (PREFIX // 3))
        def _(e):
            forward(e, True)

        x_near(part)

    for s in range(4):

        @pl.when(col != s)
        def _():
            for unit in range(2 * s + 2):
                block = lead_block(s, unit, 1 - core)
                remote(block, block, ps.at[s, unit], pr.at[s, unit], peer).wait_recv()

    @pl.when(y == 0)
    def _():
        keep_lead.wait()

    def links_of(s, t):
        index = y * 4 + (zz - s + 4) % 4
        return pick(index, [sum(1 << d for d in CHILDREN[t][a, b]) for a in range(4) for b in range(4)])

    for s in range(4):
        for unit in range(2 * s + 2):
            links = links_of(s, unit % 4)
            block = lead_block(s, unit, core)
            for d in range(4):

                @pl.when((links // (1 << d)) % 2 == 1)
                def _():
                    remote(block, block, ks.at[s, unit, d], kr.at[s, unit], around[d]).wait_send()

            @pl.when(col != s)
            def _():
                remote(block, block, ps.at[s, unit], pr.at[s, unit], peer).wait_send()

    each = (16 * (LEAD + 8) - PREFIX) // 8

    @pl.loop(0, 8)
    def _(step):
        here = pl.multiple_of(step * 128, 128)
        which = step % 2

        def hook(b):
            if b < each:
                forward(PREFIX + each * step + b, False)

        triangle128(
            lambda v: z[pl.ds(pl.multiple_of(here + 8 * v, 8), 8), pl.ds(here, 128)],
            upper,
            inverse.at[pl.ds(pl.multiple_of(which * 128, 128), 128)],
            hook,
        )
        z[pl.ds(here, 128), pl.ds(here, 128)] = upper[...]

        for k in range(4):
            o, mid, end = 256 * k, 256 * k + 128, 256 * k + 256

            @pl.when(step == 2 * k)
            def _():
                if k == 0:
                    for part in range(1, 4):
                        x_far(part)
                    for part in range(1, 4):
                        peer_take(part)
                    x_finish()

                @pl.when(row == k)
                def _():
                    top_ref[...] = z[o:end, 1024:2048]

                corner = product(split(inverse[0:128]), split(z[o:mid, mid:end]))
                z[o:mid, mid:end] = corner
                z[mid:end, mid:end] -= product(split(corner.T), split(corner))

            @pl.when(step == 2 * k + 1)
            def _():
                z[mid:end, o:mid] = jnp.zeros((128, 128), F32)
                low = inverse[128:256]
                high = inverse[0:128]
                side = product(split(z[o:mid, mid:end].T), split(high))
                side = -product(split(low), split(side))
                block = split(
                    jnp.concatenate(
                        [
                            jnp.concatenate([high, jnp.zeros((128, 128), F32)], axis=1),
                            jnp.concatenate([side, low], axis=1),
                        ],
                        axis=0,
                    )
                )
                inverse_high[k], inverse_low[k] = block
                if k < 3:
                    right = product(block, split(z[o:end, end:1024]))
                    z[o:end, end:1024] = right
                    down = split(right.T)
                    z[end:1024, end:1024] -= product(down, split(right))

                for c in range(0, 1024, TILE):
                    cols = slice(1024 + c, 1024 + c + TILE)
                    solved = product(block, split(z[o:end, cols]))
                    z[o:end, cols] = solved
                    if k < 3:
                        z[end:1024, cols] -= product(down, split(solved))

    keep_all = pltpu.make_async_copy(ar, ar_out, ls.at[6])
    keep_all.start()

    @pl.when((col < 4) & (row < 4) & (row >= col))
    def _():
        block = z[pl.ds(pl.multiple_of(jnp.minimum(col, 3) * 256, 256), 256), pl.ds(pl.multiple_of(jnp.minimum(row, 3) * 256, 256), 256)]
        top_ref[:, 0:256] = block.T

    @pl.when((col < 4) & (row < col))
    def _():
        top_ref[:, 0:256] = jnp.zeros((256, 256), F32)

    @pl.when(col < 4)
    def _():
        a = lax.broadcasted_iota(jnp.int32, (1024, 256), 0)
        b = lax.broadcasted_iota(jnp.int32, (1024, 256), 1)
        z[:, 1024:1280] = jnp.where(a == b + col * 256, -1.0, 0.0)

    for k in range(3, -1, -1):
        o, end = 256 * k, 256 * k + 256
        block = inverse_high[k].T, inverse_low[k].T
        side = split(z[o:end, end:1024]) if k < 3 else None
        for c in range(0, 1024, TILE):
            cols = slice(c, c + TILE)
            mine = z[o:end, 1024 + c : 1024 + c + TILE]
            if k < 3:
                mine = mine - product(side, (wh_ref[end:1024, cols], wl_ref[end:1024, cols]))
            wh_ref[o:end, cols], wl_ref[o:end, cols] = split(product(block, split(mine)))

    for s in range(4):
        for t in range(4):
            links = links_of(s, t)
            for d in range(4):

                @pl.when((links // (1 << d)) % 2 == 1)
                def _():
                    block = ar.at[s, pl.ds(t * 512, 512)]
                    remote(block, block, rs.at[s, t, d], rr.at[s, t, 0], around[d]).wait_send()

    keep_all.wait()


def panels(matrix):
    sems = [(4, 2), (2, 4), (2, 4), (2, 4), (4, 8, 4), (4, 8), (4, 8), (4, 8), (4, 4, 4), (4, 4, 8), (7,)]
    vmem = pl.BlockSpec(memory_space=pltpu.VMEM)
    anywhere = pl.BlockSpec(memory_space=pl.ANY)
    return pl.pallas_call(
        panels_kernel,
        out_shape=[
            jax.ShapeDtypeStruct((4, 2048, 256), F32),
            jax.ShapeDtypeStruct((1024, 1024), BF16),
            jax.ShapeDtypeStruct((1024, 1024), BF16),
            jax.ShapeDtypeStruct((256, 1024), F32),
        ],
        in_specs=[anywhere],
        out_specs=[anywhere, vmem, vmem, vmem],
        scratch_shapes=[
            pltpu.VMEM((4, 2048, 256), F32),
            pltpu.VMEM((1024, 2048), F32),
            pltpu.VMEM((256, 128), F32),
            pltpu.VMEM((128, 128), F32),
            pltpu.VMEM((4, 256, 256), BF16),
            pltpu.VMEM((4, 256, 256), BF16),
            pltpu.SMEM((16 * (LEAD + 8),), jnp.int32),
            *[pltpu.SemaphoreType.DMA(s) for s in sems],
        ],
        compiler_params=pltpu.CompilerParams(collective_id=0, has_side_effects=True, vmem_limit_bytes=56 << 20),
        name="panels",
    )(matrix)


def update_kernel(m_ref, a_ref, wh_ref, wl_ref, top_ref, out_ref):
    row, col = lax.axis_index("prow"), lax.axis_index("pcol")
    out_ref[...] = m_ref[...]

    @pl.when(col < 4)
    def _():
        out_ref[:, 0:256] = jnp.zeros((256, 256), F32)

    total = None
    for s in range(4):
        rows = slice(256 * s, 256 * s + 256)
        part = product(split(a_ref[s]), (wh_ref[rows], wl_ref[rows]))
        total = part if total is None else total + part
    out_ref[...] -= total

    @pl.when((pl.program_id(0) == 0) & (row < 4))
    def _():
        out_ref[...] = top_ref[...]


def update(matrix, column, wh, wl, top):
    tile = pl.BlockSpec((256, 1024), lambda i: (i, 0))
    whole = lambda shape: pl.BlockSpec(shape, lambda i: (0, 0))
    return pl.pallas_call(
        update_kernel,
        grid=(8,),
        out_shape=jax.ShapeDtypeStruct((2048, 1024), F32),
        in_specs=[
            tile,
            pl.BlockSpec((4, 256, 256), lambda i: (0, i, 0)),
            whole((1024, 1024)),
            whole((1024, 1024)),
            whole((256, 1024)),
        ],
        out_specs=tile,
        compiler_params=pltpu.CompilerParams(vmem_limit_bytes=60 << 20),
        name="update",
    )(matrix, column, wh, wl, top)


def shards(matrix):
    return update(matrix, *panels(matrix))


def solution(mesh):
    return jax.shard_map(
        shards,
        mesh=mesh,
        in_specs=(P("prow", "pcol"),),
        out_specs=P("prow", "pcol"),
        check_vma=False,
    )
```

```python
import functools

import jax
import jax.numpy as jnp
from jax import lax
from jax.experimental import pallas as pl
from jax.experimental.pallas import tpu as pltpu
from jax.sharding import PartitionSpec as P

F32 = jnp.float32
BF16 = jnp.bfloat16
MESH = pl.DeviceIdType.MESH

TURNS = ((1, 0), (0, -1), (-1, 0), (0, 1))
PARENT = {
    (0, 1): 0, (1, 0): 2, (0, 3): 0, (3, 0): 2, (1, 1): 2, (1, 3): 2, (3, 3): 1, (3, 1): 3,
    (1, 2): 2, (2, 3): 1, (3, 2): 3, (2, 1): 2, (2, 2): 1, (2, 0): 2, (0, 2): 0,
}


def tree_children():
    trees = []
    parent = dict(PARENT)
    for _ in range(4):
        children = {(a, b): [] for a in range(4) for b in range(4)}
        for node, turn in parent.items():
            dy, dz = TURNS[turn]
            children[(node[0] - dy) % 4, (node[1] - dz) % 4].append(turn)
        trees.append(children)
        parent = {(n[1] % 4, -n[0] % 4): (d + 1) % 4 for n, d in parent.items()}
    return trees


CHILDREN = tree_children()
UNIT = 64
ROWS = 128
COPIES = 512 // ROWS
LEAD = 2

PREFIX = 32
EARLY = 1
ORDER = (
    (
        0, 64, 128, 192, 4, 68, 132, 196, 65, 195, 69, 199, 66, 194, 70, 198, 193, 67, 129, 131,
        1, 3, 197, 71, 5, 133, 7, 135, 130, 2, 6, 134, 8, 72, 136, 200, 73, 203, 12, 76,
        140, 204, 16, 80, 144, 208, 20, 84, 148, 212, 74, 202, 77, 207, 81, 211, 9, 11, 137, 139,
        85, 215, 201, 75, 10, 138, 78, 206, 13, 15, 82, 210, 141, 143, 86, 214, 17, 205, 79, 19,
        147, 145, 209, 83, 21, 213, 87, 14, 23, 151, 149, 142, 18, 146, 22, 150,
    ),
    (
        128, 132, 129, 131, 65, 195, 133, 135, 69, 199, 0, 64, 66, 194, 192, 130, 4, 198, 68, 70,
        196, 134, 193, 1, 3, 67, 197, 71, 5, 7, 2, 6, 136, 73, 203, 137, 139, 140, 8, 72,
        200, 74, 144, 138, 148, 141, 143, 11, 9, 202, 147, 75, 145, 12, 77, 207, 151, 10, 149, 142,
        16, 201, 81, 211, 204, 78, 146, 15, 13, 20, 85, 215, 76, 150, 208, 82, 79, 19, 206, 80,
        210, 84, 14, 17, 212, 86, 214, 205, 83, 23, 209, 18, 87, 21, 213, 22,
    ),
    (
        0, 128, 4, 132, 129, 3, 1, 65, 131, 195, 133, 7, 5, 69, 135, 199, 194, 130, 66, 64,
        2, 192, 198, 70, 68, 196, 6, 134, 67, 193, 71, 197, 8, 136, 203, 11, 73, 137, 9, 139,
        12, 72, 200, 140, 10, 138, 16, 144, 15, 141, 13, 20, 148, 19, 145, 143, 14, 202, 142, 74,
        17, 149, 23, 147, 18, 146, 207, 21, 77, 151, 201, 75, 211, 22, 150, 81, 76, 215, 204, 85,
        78, 80, 208, 206, 82, 84, 212, 210, 86, 205, 79, 214, 209, 83, 213, 87,
    ),
    (
        0, 4, 1, 3, 65, 195, 5, 7, 69, 199, 128, 64, 2, 66, 192, 194, 132, 70, 68, 6,
        196, 198, 129, 67, 193, 131, 71, 133, 197, 135, 130, 134, 8, 73, 203, 9, 11, 12, 72, 200,
        202, 136, 10, 16, 13, 15, 20, 137, 201, 17, 74, 139, 19, 14, 21, 77, 207, 140, 23, 138,
        76, 206, 144, 75, 18, 81, 211, 141, 148, 204, 22, 85, 215, 205, 80, 210, 143, 145, 208, 78,
        212, 82, 214, 84, 142, 79, 209, 86, 149, 147, 83, 213, 87, 146, 151, 150,
    ),
    (
        0, 64, 128, 192, 4, 68, 132, 196, 65, 195, 69, 199, 66, 194, 70, 198, 193, 67, 129, 131,
        1, 3, 197, 71, 5, 133, 7, 135, 130, 2, 6, 134, 8, 72, 136, 200, 73, 203, 12, 76,
        140, 204, 16, 80, 144, 208, 20, 84, 148, 212, 74, 202, 77, 207, 81, 211, 9, 11, 137, 139,
        85, 215, 201, 75, 10, 138, 78, 206, 13, 15, 82, 210, 141, 143, 86, 214, 17, 205, 79, 147,
        19, 145, 209, 83, 14, 21, 213, 87, 23, 151, 149, 142, 18, 146, 22, 150,
    ),
    (
        128, 132, 129, 131, 65, 195, 133, 135, 69, 199, 0, 64, 66, 194, 192, 130, 4, 198, 68, 70,
        196, 134, 193, 1, 3, 67, 197, 71, 5, 7, 2, 6, 136, 73, 203, 137, 139, 140, 8, 72,
        200, 74, 144, 138, 148, 141, 143, 11, 9, 202, 147, 75, 145, 12, 77, 207, 151, 149, 10, 142,
        16, 201, 81, 211, 204, 78, 146, 15, 13, 20, 85, 215, 76, 150, 208, 82, 79, 19, 206, 80,
        210, 84, 14, 17, 212, 86, 214, 205, 83, 23, 209, 18, 87, 21, 213, 22,
    ),
    (
        0, 128, 4, 132, 129, 3, 1, 65, 131, 195, 133, 7, 5, 69, 135, 199, 194, 130, 66, 64,
        2, 192, 198, 70, 68, 196, 6, 134, 67, 193, 71, 197, 8, 136, 203, 11, 73, 137, 9, 139,
        12, 72, 200, 140, 10, 138, 16, 144, 15, 141, 13, 20, 148, 19, 145, 143, 14, 202, 142, 74,
        17, 149, 23, 147, 18, 146, 207, 21, 77, 151, 201, 75, 211, 22, 150, 81, 76, 215, 204, 85,
        78, 80, 208, 206, 82, 84, 212, 210, 86, 205, 79, 214, 209, 83, 213, 87,
    ),
    (
        0, 4, 1, 3, 65, 195, 5, 7, 69, 199, 128, 64, 2, 66, 192, 194, 132, 70, 68, 6,
        196, 198, 129, 67, 193, 131, 71, 133, 197, 135, 130, 134, 8, 73, 203, 9, 11, 12, 72, 200,
        202, 136, 10, 16, 13, 15, 20, 137, 201, 17, 74, 139, 19, 14, 21, 77, 207, 140, 23, 138,
        76, 206, 144, 75, 18, 81, 211, 141, 148, 204, 22, 85, 215, 205, 80, 210, 143, 145, 208, 78,
        212, 82, 214, 84, 142, 79, 209, 86, 149, 147, 83, 213, 87, 146, 151, 150,
    ),
)


def place():
    row, col = lax.axis_index("prow"), lax.axis_index("pcol")
    return row // 2, row % 2, col // 4, col % 4


def pick(index, values):
    out = jnp.int32(values[0])
    for i in range(1, len(values)):
        if values[i] != values[0] or len(set(values)) > 1:
            out = jnp.where(index == i, jnp.int32(values[i]), out)
    return out


def packed(y, code):
    dz, tree = code % 4, code // 64
    links = sum(1 << d for d in CHILDREN[tree][y, dz])
    return code + 256 * ((y == 0 and dz == 0) + 2 * links)


def split(a):
    high = a.astype(BF16)
    return high, (a - high.astype(F32)).astype(BF16)


def product(a, b):
    dot = functools.partial(jnp.dot, preferred_element_type=F32)
    return dot(a[0], b[0]) + (dot(a[0], b[1]) + dot(a[1], b[0]))


def lanes(block, j):
    return jnp.take_along_axis(block, jnp.full((8, 128), j, jnp.int32), axis=1)


def rows_of(block, i):
    return jnp.broadcast_to(block[i : i + 1], (8, 128))


def triangle128(load, upper_ref, inverse_ref, hook):
    lane = lax.broadcasted_iota(jnp.int32, (8, 128), 1)
    sub = lax.broadcasted_iota(jnp.int32, (8, 128), 0)
    strips = [load(v) for v in range(16)]
    for b in range(16):
        first, count = 8 * b, 16 - b
        inside = (lane >= first) & (lane < first + 8)
        columns = [lanes(strips[b], first + i) for i in range(8)]
        pivot = [[rows_of(columns[i], k) for k in range(8)] for i in range(8)]
        start = jnp.where(inside, jnp.where(lane == sub + first, 1.0, 0.0), strips[b])
        rows = [rows_of(start, i) for i in range(8)]
        if count > 1:
            below = [lanes(strips[b + 1], first + i) for i in range(8)]
            after = jnp.where(inside, 0.0, strips[b + 1])
        scales, factors = [], []
        for i in range(8):
            scale = 1.0 / pivot[i][i]
            scales.append(scale)
            factor = [None] * 8
            for j in range(i + 1, 8):
                factor[j] = pivot[i][j] * scale
            factors.append(factor)
            for j in range(i + 1, 8):
                pivot[j][j] = pivot[j][j] - (pivot[i][j] * pivot[i][j]) * scale
                for k in range(j + 1, 8):
                    pivot[j][k] = pivot[j][k] - factor[j] * pivot[i][k]
                rows[j] = rows[j] - factor[j] * rows[i]
            if count > 1:
                weight = below[i] * scale
                for k in range(i + 1, 8):
                    below[k] = below[k] - weight * pivot[i][k]
                after = after - weight * rows[i]
        if count > 2:
            solved = [None] * 8
            for i in range(7, -1, -1):
                row = rows[i] * scales[i]
                for k in range(i + 1, 8):
                    row = row - factors[i][k] * solved[k]
                solved[i] = row
            for v in range(2, count):
                strip = jnp.where(inside, 0.0, strips[b + v])
                for i in range(8):
                    strip = strip - lanes(strips[b + v], first + i) * solved[i]
                strips[b + v] = strip
        if count > 1:
            strips[b + 1] = after
        hook(b)
        inverse = upper = None
        for i in range(7, -1, -1):
            root = lax.rsqrt(pivot[i][i])
            left = rows[i] * root
            right = left
            for k in range(i, 8):
                right = jnp.where(lane == first + k, pivot[i][k] * root, right)
            inverse = left if inverse is None else jnp.where(sub == i, left, inverse)
            upper = right if upper is None else jnp.where(sub == i, right, upper)
        upper_ref[first : first + 8, :] = jnp.where(lane >= sub + first, upper, 0.0)
        inverse_ref[first : first + 8, :] = jnp.where(lane <= sub + first, inverse, 0.0)


TILE = 512
EXTRA = 2
HOOKS = (1, 4, 6, 8, 10, 13, 15)


def panels_kernel(
    k_ref, m, ar, wh_ref, wl_ref, top_ref, z, inverse, upper, inverse_high, inverse_low, order, xs, xr, cs, cr, ks, kr, ps, pr, rs, rr, ls
):
    x, core, y, zz = place()
    row, col = x * 2 + core, y * 4 + zz

    def at(px, pcore, py, pz):
        return (px * 2 + pcore, py * 4 + pz)

    peer = at(x, 1 - core, y, zz)
    after, before, across = (at((x + d) % 4, core, y, zz) for d in (1, 3, 2))
    around = [at(x, core, (y + dy + 4) % 4, (zz + dz + 4) % 4) for dy, dz in TURNS]
    barrier = pltpu.get_barrier_semaphore()
    for device in [peer, after, before, across, *around]:
        pl.semaphore_signal(barrier, inc=1, device_id=device, device_id_type=MESH)

    def top_rows(o, of_core, part):
        return z.at[pl.ds(pl.multiple_of(o * 512 + of_core * 256, 256), 256), pl.ds(1024 + 256 * part, 256)]

    def own_top(part):
        return k_ref.at[pl.ds(0, 256), pl.ds(256 * part, 256)]

    def x_keep(o, part):
        return pltpu.make_async_copy(own_top(part), top_rows(o, core, part), ls.at[part])

    for o in range(2):

        @pl.when(x == o)
        def _():
            for part in range(4):
                x_keep(o, part).start()

    keep_column = pltpu.make_async_copy(k_ref.at[:, pl.ds(0, 256)], ar.at[zz], ls.at[4])
    keep_block = pltpu.make_async_copy(k_ref, m, ls.at[6])

    @pl.when(y == 0)
    def _():
        keep_column.start()

    for e in range(16 * (LEAD + COPIES)):
        order[e] = pick(y + 4 * (x // 2), [packed(i % 4, ORDER[i][e]) for i in range(8)])

    pl.semaphore_wait(barrier, 8)

    def remote(src, dst, ssem, rsem, device):
        return pltpu.make_async_remote_copy(src, dst, ssem, rsem, device_id=device, device_id_type=MESH)

    def x_own(o, part, i):
        block = top_rows(o, core, part)
        return remote(block, block, xs.at[part, i], xr.at[o, part], (after, before, across)[i])

    def x_pass(o, part, device):
        block = top_rows(o, core, part)
        return remote(block, block, xs.at[part, 0], xr.at[o, part], device)

    def peer_own(o, part):
        block = top_rows(o, core, part)
        return remote(block, block, cs.at[o, part], cr.at[o, part], peer)

    def peer_pass(o, part, of_core):
        block = top_rows(o, of_core, part)
        return remote(block, block, cs.at[o, part], cr.at[o, part], peer)

    def x_start(part):
        for o in range(2):

            @pl.when(x == o)
            def _():
                x_keep(o, part).wait()
                x_own(o, part, 0).start()
                x_own(o, part, 1).start()
                if part == 0:
                    x_own(o, part, 2).start()
                peer_own(o, part).start()

    def x_near(part):
        for o in range(2):

            @pl.when(x == 1 - o)
            def _():
                x_pass(o, part, peer).wait_recv()
                peer_pass(o, part, core).start()

        for near, mine, device in ((1, 2, after), (0, 3, before)):

            @pl.when(x == mine)
            def _():
                x_pass(near, part, device).wait_recv()
                if part > 0:
                    x_pass(near, part, device).start()
                peer_pass(near, part, core).start()

    def x_far(part):
        for far, mine in ((0, 2), (1, 3)):

            @pl.when(x == mine)
            def _():
                x_pass(far, part, peer).wait_recv()
                peer_pass(far, part, core).start()

    def peer_take(part):
        for o in range(2):
            peer_pass(o, part, 1 - core).wait_recv()

    def x_finish():
        for part in range(4):
            for o in range(2):

                @pl.when(x == o)
                def _():
                    x_own(o, part, 0).wait_send()
                    x_own(o, part, 1).wait_send()
                    if part == 0:
                        x_own(o, part, 2).wait_send()
                    peer_own(o, part).wait_send()
                    peer_pass(1 - o, part, core).wait_send()

            @pl.when(x >= 2)
            def _():
                if part > 0:
                    x_pass(0, part, peer).wait_send()
                for o in range(2):
                    peer_pass(o, part, core).wait_send()

    def lead_block(s, unit, of_core):
        start = pl.multiple_of((unit // 2) * 256 + of_core * 128 + (unit % 2) * UNIT, UNIT)
        return z.at[pl.ds(start, UNIT), pl.ds(pl.multiple_of(s * 256, 256), 256)]

    def lead_root(unit):
        start = pl.multiple_of((unit // 2) * 256 + core * 128 + (unit % 2) * UNIT, UNIT)
        return z.at[pl.ds(start, UNIT), pl.ds(1024, 256)]

    def row_block(s, t, q):
        return ar.at[s, pl.ds(pl.multiple_of(t * 512 + q * ROWS, ROWS), ROWS)]

    def forward(e, leading):
        code = order[e]
        s = (zz - code % 4 + 4) % 4
        q = (code // 4) % 16
        t = (code // 64) % 4
        root = (code // 256) % 2
        links = code // 512
        flags = [(links // (1 << d)) % 2 == 1 for d in range(4)]
        if leading:
            unit = q * 4 + t
            lead = (q < LEAD) & (unit // 2 <= s)

            @pl.when(lead & (root == 1))
            def _():
                for d in range(4):

                    @pl.when(flags[d])
                    def _():
                        remote(lead_root(unit), lead_block(s, unit, core), ks.at[s, unit, d], kr.at[s, unit], around[d]).start()

            @pl.when(lead & (root == 0))
            def _():
                block = lead_block(s, unit, core)
                remote(block, block, ps.at[s, unit], kr.at[s, unit], peer).wait_recv()
                for d in range(4):

                    @pl.when(flags[d])
                    def _():
                        remote(block, block, ks.at[s, unit, d], kr.at[s, unit], around[d]).start()

                remote(block, block, ps.at[s, unit], pr.at[s, unit], peer).start()

        def pass_row():
            n = q - LEAD
            block = row_block(s, t, n)

            @pl.when(root == 0)
            def _():
                remote(block, block, rs.at[s, t, 0], rr.at[s, t, n], peer).wait_recv()

            for d in range(4):

                @pl.when(flags[d] & ((root == 0) | (n >= EARLY)))
                def _():
                    remote(block, block, rs.at[s, t, d], rr.at[s, t, n], around[d]).start()

        if leading:
            pl.when(q >= LEAD)(pass_row)
        else:
            pass_row()

    keep_lead = pltpu.make_async_copy(z.at[:, pl.ds(1024, 256)], z.at[:, pl.ds(pl.multiple_of(zz * 256, 256), 256)], ls.at[5])

    def x_first():
        x_near(0)
        x_far(0)
        peer_take(0)

    x_start(0)

    @pl.when(y == 0)
    def _():
        keep_column.wait()
        for q in range(EARLY):
            for t in range(4):
                (d,) = CHILDREN[t][0, 0]
                block = row_block(zz, t, q)
                remote(block, block, rs.at[zz, t, d], rr.at[zz, t, q], around[d]).start()

        x_first()
        keep_lead.start()

    for part in range(1, 4):
        x_start(part)

    for part in range(1, 4):

        @pl.loop(PREFIX * (part - 1) // 3, PREFIX * part // 3)
        def _(e):
            forward(e, True)

        if part == 1:
            pl.when(y != 0)(x_first)
        x_near(part)

    for s in range(4):

        @pl.when(col != s)
        def _():
            for unit in range(2 * s + 2):
                block = lead_block(s, unit, 1 - core)
                remote(block, block, ps.at[s, unit], pr.at[s, unit], peer).wait_recv()

    @pl.when(y == 0)
    def _():
        keep_lead.wait()

    keep_block.start()

    def links_of(s, t):
        index = y * 4 + (zz - s + 4) % 4
        return pick(index, [sum(1 << d for d in CHILDREN[t][a, b]) for a in range(4) for b in range(4)])

    for s in range(4):
        for unit in range(2 * s + 2):
            links = links_of(s, unit % 4)
            block = lead_block(s, unit, core)
            for d in range(4):

                @pl.when((links // (1 << d)) % 2 == 1)
                def _():
                    remote(block, block, ks.at[s, unit, d], kr.at[s, unit], around[d]).wait_send()

            @pl.when(col != s)
            def _():
                remote(block, block, ps.at[s, unit], pr.at[s, unit], peer).wait_send()


    @pl.loop(0, 8)
    def _(step):
        here = pl.multiple_of(step * 128, 128)
        which = step % 2

        def hook(b):
            if b in HOOKS:
                forward(PREFIX + len(HOOKS) * step + EXTRA * (step // 2) + HOOKS.index(b), False)

        triangle128(
            lambda v: z[pl.ds(pl.multiple_of(here + 8 * v, 8), 8), pl.ds(here, 128)],
            upper,
            inverse.at[pl.ds(pl.multiple_of(which * 128, 128), 128)],
            hook,
        )
        z[pl.ds(here, 128), pl.ds(here, 128)] = upper[...]

        for k in range(4):
            o, mid, end = 256 * k, 256 * k + 128, 256 * k + 256

            @pl.when(step == 2 * k)
            def _():
                corner = product(split(inverse[0:128]), split(z[o:mid, mid:end]))
                z[o:mid, mid:end] = corner
                z[mid:end, mid:end] -= product(split(corner.T), split(corner))

            @pl.when(step == 2 * k + 1)
            def _():
                z[mid:end, o:mid] = jnp.zeros((128, 128), F32)
                spare = iter(range(PREFIX + (2 * len(HOOKS) + EXTRA) * k + 2 * len(HOOKS), PREFIX + (2 * len(HOOKS) + EXTRA) * (k + 1)))

                def between(count):
                    for e in [e for _, e in zip(range(count), spare)]:
                        forward(jnp.int32(e), False)

                low = inverse[128:256]
                high = inverse[0:128]
                side = product(split(z[o:mid, mid:end].T), split(high))
                side = -product(split(low), split(side))
                block = split(
                    jnp.concatenate(
                        [
                            jnp.concatenate([high, jnp.zeros((128, 128), F32)], axis=1),
                            jnp.concatenate([side, low], axis=1),
                        ],
                        axis=0,
                    )
                )
                inverse_high[k], inverse_low[k] = block
                between(1)
                if k < 3:
                    right = product(block, split(z[o:end, end:1024]))
                    z[o:end, end:1024] = right
                    down = split(right.T)
                    z[end:1024, end:1024] -= product(down, split(right))
                between(1)

                if k == 0:
                    for part in range(1, 4):
                        x_far(part)
                    for part in range(1, 4):
                        peer_take(part)
                    x_finish()

                @pl.when(row == k)
                def _():
                    top_ref[...] = z[o:end, 1024:2048]

                for c in range(0, 1024, TILE):
                    cols = slice(1024 + c, 1024 + c + TILE)
                    solved = product(block, split(z[o:end, cols]))
                    z[o:end, cols] = solved
                    if k < 3:
                        z[end:1024, cols] -= product(down, split(solved))
                    between(1 if c == 0 else EXTRA)

    @pl.when((col < 4) & (row < 4) & (row >= col))
    def _():
        block = z[pl.ds(pl.multiple_of(jnp.minimum(col, 3) * 256, 256), 256), pl.ds(pl.multiple_of(jnp.minimum(row, 3) * 256, 256), 256)]
        top_ref[:, 0:256] = block.T

    @pl.when((col < 4) & (row < col))
    def _():
        top_ref[:, 0:256] = jnp.zeros((256, 256), F32)

    @pl.when(col < 4)
    def _():
        a = lax.broadcasted_iota(jnp.int32, (1024, 256), 0)
        b = lax.broadcasted_iota(jnp.int32, (1024, 256), 1)
        z[:, 1024:1280] = jnp.where(a == b + col * 256, -1.0, 0.0)

    for k in range(3, -1, -1):
        o, end = 256 * k, 256 * k + 256
        block = inverse_high[k].T, inverse_low[k].T
        side = split(z[o:end, end:1024]) if k < 3 else None
        for c in range(0, 1024, TILE):
            cols = slice(c, c + TILE)
            mine = z[o:end, 1024 + c : 1024 + c + TILE]
            if k < 3:
                mine = mine - product(side, (wh_ref[end:1024, cols], wl_ref[end:1024, cols]))
            wh_ref[o:end, cols], wl_ref[o:end, cols] = split(product(block, split(mine)))

    keep_block.wait()

    @pl.when(col < 4)
    def _():
        m[:, 0:256] = jnp.zeros((2048, 256), F32)

    @pl.loop(PREFIX + 8 * len(HOOKS) + 4 * EXTRA, 16 * (LEAD + COPIES))
    def _(e):
        forward(e, False)

    for s in range(4):
        for t in range(4):
            links = links_of(s, t)
            for d in range(4):

                @pl.when((links // (1 << d)) % 2 == 1)
                def _():
                    block = ar.at[s, pl.ds(t * 512, 512)]
                    remote(block, block, rs.at[s, t, d], rr.at[s, t, 0], around[d]).wait_send()


def panels(matrix):
    sems = [(4, 3), (2, 4), (2, 4), (2, 4), (4, 8, 4), (4, 8), (4, 8), (4, 8), (4, 4, 4), (4, 4, COPIES), (7,)]
    return pl.pallas_call(
        panels_kernel,
        out_shape=[
            jax.ShapeDtypeStruct((2048, 1024), F32),
            jax.ShapeDtypeStruct((4, 2048, 256), F32),
            jax.ShapeDtypeStruct((1024, 1024), BF16),
            jax.ShapeDtypeStruct((1024, 1024), BF16),
            jax.ShapeDtypeStruct((256, 1024), F32),
        ],
        in_specs=[pl.BlockSpec(memory_space=pl.ANY)],
        out_specs=[pl.BlockSpec(memory_space=pltpu.VMEM)] * 5,
        scratch_shapes=[
            pltpu.VMEM((1024, 2048), F32),
            pltpu.VMEM((256, 128), F32),
            pltpu.VMEM((128, 128), F32),
            pltpu.VMEM((4, 256, 256), BF16),
            pltpu.VMEM((4, 256, 256), BF16),
            pltpu.SMEM((16 * (LEAD + COPIES),), jnp.int32),
            *[pltpu.SemaphoreType.DMA(s) for s in sems],
        ],
        compiler_params=pltpu.CompilerParams(collective_id=0, has_side_effects=True, vmem_limit_bytes=26 << 20),
        name="panels",
    )(matrix)


def update_kernel(m, ar, wh, wl, top, out):
    i = pl.program_id(0)
    rows = pl.ds(pl.multiple_of(i * 256, 256), 256)
    total = m[rows]
    left = split(jnp.concatenate([ar[s, rows] for s in range(4)], axis=1))
    out[...] = total - product(left, (wh[...], wl[...]))

    @pl.when((i == 0) & (lax.axis_index("prow") < 4))
    def _():
        out[...] = top[...]


def shards(matrix):
    return pl.pallas_call(
        update_kernel,
        grid=(8,),
        out_shape=jax.ShapeDtypeStruct((2048, 1024), F32),
        in_specs=[pl.BlockSpec(memory_space=pltpu.VMEM)] * 5,
        out_specs=pl.BlockSpec((256, 1024), lambda i: (i, 0)),
        compiler_params=pltpu.CompilerParams(vmem_limit_bytes=20 << 20),
        name="update",
    )(*panels(matrix))


def solution(mesh):
    return jax.shard_map(
        shards,
        mesh=mesh,
        in_specs=(P("prow", "pcol"),),
        out_specs=P("prow", "pcol"),
        check_vma=False,
    )
```

```python
import functools

import jax
import jax.numpy as jnp
from jax import lax
from jax.experimental import pallas as pl
from jax.experimental.pallas import tpu as pltpu
from jax.sharding import PartitionSpec as P

F32 = jnp.float32
BF16 = jnp.bfloat16
MESH = pl.DeviceIdType.MESH

TURNS = ((1, 0), (0, -1), (-1, 0), (0, 1))
PARENT = {
    (0, 1): 0, (1, 0): 2, (0, 3): 0, (3, 0): 2, (1, 1): 2, (1, 3): 2, (3, 3): 1, (3, 1): 3,
    (1, 2): 2, (2, 3): 1, (3, 2): 3, (2, 1): 2, (2, 2): 1, (2, 0): 2, (0, 2): 0,
}


def tree_children():
    trees = []
    parent = dict(PARENT)
    for _ in range(4):
        children = {(a, b): [] for a in range(4) for b in range(4)}
        for node, turn in parent.items():
            dy, dz = TURNS[turn]
            children[(node[0] - dy) % 4, (node[1] - dz) % 4].append(turn)
        trees.append(children)
        parent = {(n[1] % 4, -n[0] % 4): (d + 1) % 4 for n, d in parent.items()}
    return trees


CHILDREN = tree_children()
UNIT = 64
ROWS = 128
COPIES = 512 // ROWS
LEAD = 2

PREFIX = 32
EARLY = 2
ORDER = (
    (
        0, 64, 128, 192, 4, 68, 132, 196, 65, 195, 69, 199, 66, 194, 70, 198, 193, 67, 129, 131,
        1, 3, 197, 71, 5, 133, 7, 135, 130, 2, 6, 134, 8, 72, 136, 200, 12, 76, 140, 204,
        73, 203, 77, 207, 16, 80, 144, 208, 20, 84, 148, 212, 74, 202, 78, 206, 81, 211, 9, 11,
        137, 139, 85, 215, 201, 75, 13, 15, 141, 143, 205, 79, 10, 82, 210, 138, 14, 86, 214, 142,
        209, 83, 17, 147, 213, 87, 19, 145, 21, 151, 23, 149, 18, 146, 22, 150,
    ),
    (
        128, 132, 129, 131, 65, 195, 133, 135, 69, 199, 0, 64, 66, 194, 192, 130, 4, 198, 68, 70,
        196, 134, 193, 1, 3, 67, 197, 71, 5, 7, 2, 6, 136, 140, 73, 203, 137, 139, 141, 143,
        8, 77, 207, 72, 12, 200, 74, 144, 11, 138, 148, 142, 204, 78, 9, 76, 202, 15, 206, 147,
        10, 75, 13, 145, 151, 81, 211, 201, 149, 14, 16, 79, 205, 85, 215, 146, 20, 208, 82, 210,
        19, 80, 150, 214, 86, 212, 17, 23, 84, 18, 83, 209, 213, 87, 21, 22,
    ),
    (
        0, 128, 4, 132, 129, 3, 1, 65, 131, 195, 133, 7, 5, 69, 135, 199, 194, 130, 66, 64,
        2, 192, 198, 70, 68, 196, 6, 134, 67, 193, 71, 197, 8, 136, 12, 140, 11, 137, 203, 73,
        9, 15, 141, 10, 139, 13, 138, 143, 200, 72, 207, 77, 14, 142, 16, 144, 76, 204, 20, 148,
        19, 145, 74, 202, 149, 23, 17, 206, 78, 18, 147, 75, 146, 201, 21, 211, 81, 151, 22, 150,
        205, 79, 215, 85, 80, 208, 82, 210, 84, 212, 86, 214, 209, 83, 213, 87,
    ),
    (
        0, 4, 1, 3, 65, 195, 5, 7, 69, 199, 128, 64, 2, 66, 192, 194, 132, 70, 68, 6,
        196, 198, 129, 67, 193, 131, 71, 133, 197, 135, 130, 134, 8, 12, 73, 203, 9, 11, 13, 15,
        77, 207, 136, 200, 72, 202, 10, 140, 16, 137, 14, 20, 76, 206, 204, 141, 74, 139, 201, 17,
        78, 19, 21, 138, 143, 81, 211, 75, 23, 205, 142, 18, 79, 85, 215, 144, 80, 210, 148, 22,
        82, 208, 145, 86, 214, 84, 149, 212, 209, 147, 83, 146, 213, 87, 151, 150,
    ),
    (
        0, 64, 128, 192, 4, 68, 132, 196, 65, 195, 69, 199, 66, 194, 70, 198, 193, 67, 129, 131,
        1, 3, 197, 71, 5, 133, 7, 135, 130, 2, 6, 134, 8, 72, 136, 200, 12, 76, 140, 204,
        73, 203, 77, 207, 16, 80, 144, 208, 20, 84, 148, 212, 74, 202, 78, 206, 81, 211, 9, 11,
        137, 139, 85, 215, 201, 75, 13, 15, 141, 143, 205, 79, 10, 82, 210, 138, 14, 86, 214, 142,
        209, 83, 17, 147, 213, 87, 19, 145, 21, 151, 23, 149, 18, 146, 22, 150,
    ),
    (
        128, 132, 129, 131, 65, 195, 133, 135, 69, 199, 0, 64, 66, 194, 192, 130, 4, 198, 68, 70,
        196, 134, 193, 1, 3, 67, 197, 71, 5, 7, 2, 6, 136, 140, 73, 203, 137, 139, 141, 143,
        8, 77, 207, 72, 12, 200, 74, 144, 11, 138, 148, 142, 204, 78, 9, 76, 202, 15, 206, 147,
        10, 75, 13, 145, 151, 81, 211, 201, 149, 14, 16, 79, 205, 85, 215, 146, 20, 208, 82, 210,
        19, 80, 150, 214, 86, 212, 17, 23, 84, 18, 83, 209, 213, 87, 21, 22,
    ),
    (
        0, 128, 4, 132, 129, 3, 1, 65, 131, 195, 133, 7, 5, 69, 135, 199, 194, 130, 66, 64,
        2, 192, 198, 70, 68, 196, 6, 134, 67, 193, 71, 197, 8, 136, 12, 140, 11, 137, 203, 73,
        9, 15, 141, 10, 139, 13, 138, 143, 200, 72, 207, 77, 14, 142, 16, 144, 76, 204, 20, 148,
        19, 145, 74, 202, 149, 23, 17, 206, 78, 18, 147, 75, 146, 201, 21, 211, 81, 151, 22, 150,
        205, 79, 215, 85, 80, 208, 82, 210, 84, 212, 86, 214, 209, 83, 213, 87,
    ),
    (
        0, 4, 1, 3, 65, 195, 5, 7, 69, 199, 128, 64, 2, 66, 192, 194, 132, 70, 68, 6,
        196, 198, 129, 67, 193, 131, 71, 133, 197, 135, 130, 134, 8, 12, 73, 203, 9, 11, 13, 15,
        77, 207, 136, 200, 72, 202, 10, 140, 16, 137, 14, 20, 76, 206, 204, 141, 74, 139, 201, 17,
        78, 19, 21, 138, 143, 81, 211, 75, 23, 205, 142, 18, 79, 85, 215, 144, 80, 210, 148, 22,
        82, 208, 145, 86, 214, 84, 149, 212, 209, 147, 83, 146, 213, 87, 151, 150,
    ),
)


def place():
    row, col = lax.axis_index("prow"), lax.axis_index("pcol")
    return row // 2, row % 2, col // 4, col % 4


def pick(index, values):
    out = jnp.int32(values[0])
    for i in range(1, len(values)):
        if values[i] != values[0] or len(set(values)) > 1:
            out = jnp.where(index == i, jnp.int32(values[i]), out)
    return out


def packed(y, code):
    dz, tree = code % 4, code // 64
    links = sum(1 << d for d in CHILDREN[tree][y, dz])
    return code + 256 * ((y == 0 and dz == 0) + 2 * links)


def split(a):
    high = a.astype(BF16)
    return high, (a - high.astype(F32)).astype(BF16)


def product(a, b):
    dot = functools.partial(jnp.dot, preferred_element_type=F32)
    return dot(a[0], b[0]) + (dot(a[0], b[1]) + dot(a[1], b[0]))


def lanes(block, j):
    return jnp.take_along_axis(block, jnp.full((8, 128), j, jnp.int32), axis=1)


def rows_of(block, i):
    return jnp.broadcast_to(block[i : i + 1], (8, 128))


def triangle128(load, upper_ref, inverse_ref, hook):
    lane = lax.broadcasted_iota(jnp.int32, (8, 128), 1)
    sub = lax.broadcasted_iota(jnp.int32, (8, 128), 0)
    strips = [load(v) for v in range(16)]
    for b in range(16):
        first, count = 8 * b, 16 - b
        inside = (lane >= first) & (lane < first + 8)
        columns = [lanes(strips[b], first + i) for i in range(8)]
        pivot = [[rows_of(columns[i], k) for k in range(8)] for i in range(8)]
        start = jnp.where(inside, jnp.where(lane == sub + first, 1.0, 0.0), strips[b])
        rows = [rows_of(start, i) for i in range(8)]
        if count > 1:
            below = [lanes(strips[b + 1], first + i) for i in range(8)]
            after = jnp.where(inside, 0.0, strips[b + 1])
        scales, factors = [], []
        for i in range(8):
            scale = 1.0 / pivot[i][i]
            scales.append(scale)
            factor = [None] * 8
            for j in range(i + 1, 8):
                factor[j] = pivot[i][j] * scale
            factors.append(factor)
            for j in range(i + 1, 8):
                pivot[j][j] = pivot[j][j] - (pivot[i][j] * pivot[i][j]) * scale
                for k in range(j + 1, 8):
                    pivot[j][k] = pivot[j][k] - factor[j] * pivot[i][k]
                rows[j] = rows[j] - factor[j] * rows[i]
            if count > 1:
                weight = below[i] * scale
                for k in range(i + 1, 8):
                    below[k] = below[k] - weight * pivot[i][k]
                after = after - weight * rows[i]
        if count > 2:
            solved = [None] * 8
            for i in range(7, -1, -1):
                row = rows[i] * scales[i]
                for k in range(i + 1, 8):
                    row = row - factors[i][k] * solved[k]
                solved[i] = row
            for v in range(2, count):
                strip = jnp.where(inside, 0.0, strips[b + v])
                for i in range(8):
                    strip = strip - lanes(strips[b + v], first + i) * solved[i]
                strips[b + v] = strip
        if count > 1:
            strips[b + 1] = after
        hook(b)
        inverse = upper = None
        for i in range(7, -1, -1):
            root = lax.rsqrt(pivot[i][i])
            left = rows[i] * root
            right = left
            for k in range(i, 8):
                right = jnp.where(lane == first + k, pivot[i][k] * root, right)
            inverse = left if inverse is None else jnp.where(sub == i, left, inverse)
            upper = right if upper is None else jnp.where(sub == i, right, upper)
        upper_ref[first : first + 8, :] = jnp.where(lane >= sub + first, upper, 0.0)
        inverse_ref[first : first + 8, :] = jnp.where(lane <= sub + first, inverse, 0.0)


TILE = 512
EXTRA = 4
HOOKS = (2, 4, 7, 10, 12, 15)


def panels_kernel(
    k_ref, m, ar, wh_ref, wl_ref, top_ref, z, inverse, upper, inverse_high, inverse_low, order, xs, xr, cs, cr, ks, kr, ps, pr, rs, rr, ls
):
    x, core, y, zz = place()
    row, col = x * 2 + core, y * 4 + zz

    def at(px, pcore, py, pz):
        return (px * 2 + pcore, py * 4 + pz)

    peer = at(x, 1 - core, y, zz)
    after, before, across = (at((x + d) % 4, core, y, zz) for d in (1, 3, 2))
    around = [at(x, core, (y + dy + 4) % 4, (zz + dz + 4) % 4) for dy, dz in TURNS]
    barrier = pltpu.get_barrier_semaphore()
    for device in [peer, after, before, across, *around]:
        pl.semaphore_signal(barrier, inc=1, device_id=device, device_id_type=MESH)

    def top_rows(o, of_core, part):
        return z.at[pl.ds(pl.multiple_of(o * 512 + of_core * 256, 256), 256), pl.ds(1024 + 256 * part, 256)]

    def own_top(part):
        return k_ref.at[pl.ds(0, 256), pl.ds(256 * part, 256)]

    def x_keep(o, part):
        return pltpu.make_async_copy(own_top(part), top_rows(o, core, part), ls.at[part])

    for o in range(2):

        @pl.when(x == o)
        def _():
            for part in range(4):
                x_keep(o, part).start()

    keep_column = pltpu.make_async_copy(k_ref.at[:, pl.ds(0, 256)], ar.at[zz], ls.at[4])
    keep_block = pltpu.make_async_copy(k_ref, m, ls.at[6])

    @pl.when(y == 0)
    def _():
        keep_column.start()

    for e in range(16 * (LEAD + COPIES)):
        order[e] = pick(y + 4 * (x // 2), [packed(i % 4, ORDER[i][e]) for i in range(8)])

    pl.semaphore_wait(barrier, 8)

    def remote(src, dst, ssem, rsem, device):
        return pltpu.make_async_remote_copy(src, dst, ssem, rsem, device_id=device, device_id_type=MESH)

    def x_own(o, part, i):
        block = top_rows(o, core, part)
        return remote(block, block, xs.at[part, i], xr.at[o, part], (after, before, across)[i])

    def x_pass(o, part, device):
        block = top_rows(o, core, part)
        return remote(block, block, xs.at[part, 0], xr.at[o, part], device)

    def peer_own(o, part):
        block = top_rows(o, core, part)
        return remote(block, block, cs.at[o, part], cr.at[o, part], peer)

    def peer_pass(o, part, of_core):
        block = top_rows(o, of_core, part)
        return remote(block, block, cs.at[o, part], cr.at[o, part], peer)

    def x_start(part):
        for o in range(2):

            @pl.when(x == o)
            def _():
                x_keep(o, part).wait()
                x_own(o, part, 0).start()
                x_own(o, part, 1).start()
                if part == 0:
                    x_own(o, part, 2).start()
                peer_own(o, part).start()

    def x_near(part):
        for o in range(2):

            @pl.when(x == 1 - o)
            def _():
                x_pass(o, part, peer).wait_recv()
                peer_pass(o, part, core).start()

        for near, mine, device in ((1, 2, after), (0, 3, before)):

            @pl.when(x == mine)
            def _():
                x_pass(near, part, device).wait_recv()
                if part > 0:
                    x_pass(near, part, device).start()
                peer_pass(near, part, core).start()

    def x_far(part):
        for far, mine in ((0, 2), (1, 3)):

            @pl.when(x == mine)
            def _():
                x_pass(far, part, peer).wait_recv()
                peer_pass(far, part, core).start()

    def peer_take(part):
        for o in range(2):
            peer_pass(o, part, 1 - core).wait_recv()

    def x_finish():
        for part in range(4):
            for o in range(2):

                @pl.when(x == o)
                def _():
                    x_own(o, part, 0).wait_send()
                    x_own(o, part, 1).wait_send()
                    if part == 0:
                        x_own(o, part, 2).wait_send()
                    peer_own(o, part).wait_send()
                    peer_pass(1 - o, part, core).wait_send()

            @pl.when(x >= 2)
            def _():
                if part > 0:
                    x_pass(0, part, peer).wait_send()
                for o in range(2):
                    peer_pass(o, part, core).wait_send()

    def lead_block(s, unit, of_core):
        start = pl.multiple_of((unit // 2) * 256 + of_core * 128 + (unit % 2) * UNIT, UNIT)
        return z.at[pl.ds(start, UNIT), pl.ds(pl.multiple_of(s * 256, 256), 256)]

    def lead_root(unit):
        start = pl.multiple_of((unit // 2) * 256 + core * 128 + (unit % 2) * UNIT, UNIT)
        return z.at[pl.ds(start, UNIT), pl.ds(1024, 256)]

    def row_block(s, t, q):
        return ar.at[s, pl.ds(pl.multiple_of(t * 512 + q * ROWS, ROWS), ROWS)]

    def forward(e, leading):
        code = order[e]
        s = (zz - code % 4 + 4) % 4
        q = (code // 4) % 16
        t = (code // 64) % 4
        root = (code // 256) % 2
        links = code // 512
        flags = [(links // (1 << d)) % 2 == 1 for d in range(4)]
        if leading:
            unit = q * 4 + t
            lead = (q < LEAD) & (unit // 2 <= s)

            @pl.when(lead & (root == 1))
            def _():
                for d in range(4):

                    @pl.when(flags[d])
                    def _():
                        remote(lead_root(unit), lead_block(s, unit, core), ks.at[s, unit, d], kr.at[s, unit], around[d]).start()

            @pl.when(lead & (root == 0))
            def _():
                block = lead_block(s, unit, core)
                remote(block, block, ps.at[s, unit], kr.at[s, unit], peer).wait_recv()
                for d in range(4):

                    @pl.when(flags[d])
                    def _():
                        remote(block, block, ks.at[s, unit, d], kr.at[s, unit], around[d]).start()

                remote(block, block, ps.at[s, unit], pr.at[s, unit], peer).start()

        def pass_row():
            n = q - LEAD
            block = row_block(s, t, n)

            @pl.when(root == 0)
            def _():
                remote(block, block, rs.at[s, t, 0], rr.at[s, t, n], peer).wait_recv()

            for d in range(4):

                @pl.when(flags[d] & ((root == 0) | (n >= EARLY)))
                def _():
                    remote(block, block, rs.at[s, t, d], rr.at[s, t, n], around[d]).start()

        if leading:
            pl.when(q >= LEAD)(pass_row)
        else:
            pass_row()

    keep_lead = pltpu.make_async_copy(z.at[:, pl.ds(1024, 256)], z.at[:, pl.ds(pl.multiple_of(zz * 256, 256), 256)], ls.at[5])

    def x_first():
        x_near(0)
        x_far(0)
        peer_take(0)

    x_start(0)

    @pl.when(y == 0)
    def _():
        keep_column.wait()
        for q in range(EARLY):
            for t in range(4):
                (d,) = CHILDREN[t][0, 0]
                block = row_block(zz, t, q)
                remote(block, block, rs.at[zz, t, d], rr.at[zz, t, q], around[d]).start()

        x_first()
        keep_lead.start()

    for part in range(1, 4):
        x_start(part)

    for part in range(1, 4):

        @pl.loop(PREFIX * (part - 1) // 3, PREFIX * part // 3)
        def _(e):
            forward(e, True)

        if part == 1:
            pl.when(y != 0)(x_first)
        x_near(part)

    for s in range(4):

        @pl.when(col != s)
        def _():
            for unit in range(2 * s + 2):
                block = lead_block(s, unit, 1 - core)
                remote(block, block, ps.at[s, unit], pr.at[s, unit], peer).wait_recv()

    @pl.when(y == 0)
    def _():
        keep_lead.wait()

    keep_block.start()

    def links_of(s, t):
        index = y * 4 + (zz - s + 4) % 4
        return pick(index, [sum(1 << d for d in CHILDREN[t][a, b]) for a in range(4) for b in range(4)])

    for s in range(4):
        for unit in range(2 * s + 2):
            links = links_of(s, unit % 4)
            block = lead_block(s, unit, core)
            for d in range(4):

                @pl.when((links // (1 << d)) % 2 == 1)
                def _():
                    remote(block, block, ks.at[s, unit, d], kr.at[s, unit], around[d]).wait_send()

            @pl.when(col != s)
            def _():
                remote(block, block, ps.at[s, unit], pr.at[s, unit], peer).wait_send()


    @pl.loop(0, 8)
    def _(step):
        here = pl.multiple_of(step * 128, 128)
        which = step % 2

        def hook(b):
            if b in HOOKS:
                forward(PREFIX + len(HOOKS) * step + EXTRA * (step // 2) + HOOKS.index(b), False)

        triangle128(
            lambda v: z[pl.ds(pl.multiple_of(here + 8 * v, 8), 8), pl.ds(here, 128)],
            upper,
            inverse.at[pl.ds(pl.multiple_of(which * 128, 128), 128)],
            hook,
        )
        z[pl.ds(here, 128), pl.ds(here, 128)] = upper[...]

        for k in range(4):
            o, mid, end = 256 * k, 256 * k + 128, 256 * k + 256

            @pl.when(step == 2 * k)
            def _():
                corner = product(split(inverse[0:128]), split(z[o:mid, mid:end]))
                z[o:mid, mid:end] = corner
                z[mid:end, mid:end] -= product(split(corner.T), split(corner))

            @pl.when(step == 2 * k + 1)
            def _():
                z[mid:end, o:mid] = jnp.zeros((128, 128), F32)
                spare = iter(range(PREFIX + (2 * len(HOOKS) + EXTRA) * k + 2 * len(HOOKS), PREFIX + (2 * len(HOOKS) + EXTRA) * (k + 1)))

                def between(count):
                    for e in [e for _, e in zip(range(count), spare)]:
                        forward(jnp.int32(e), False)

                low = inverse[128:256]
                high = inverse[0:128]
                side = product(split(z[o:mid, mid:end].T), split(high))
                side = -product(split(low), split(side))
                block = split(
                    jnp.concatenate(
                        [
                            jnp.concatenate([high, jnp.zeros((128, 128), F32)], axis=1),
                            jnp.concatenate([side, low], axis=1),
                        ],
                        axis=0,
                    )
                )
                inverse_high[k], inverse_low[k] = block
                between(1)
                if k < 3:
                    right = product(block, split(z[o:end, end:1024]))
                    z[o:end, end:1024] = right
                    down = split(right.T)
                    z[end:1024, end:1024] -= product(down, split(right))
                between(1)

                if k == 0:
                    for part in range(1, 4):
                        x_far(part)
                    for part in range(1, 4):
                        peer_take(part)
                    x_finish()

                @pl.when(row == k)
                def _():
                    top_ref[...] = z[o:end, 1024:2048]

                for c in range(0, 1024, TILE):
                    cols = slice(1024 + c, 1024 + c + TILE)
                    solved = product(block, split(z[o:end, cols]))
                    z[o:end, cols] = solved
                    if k < 3:
                        z[end:1024, cols] -= product(down, split(solved))
                    between(1 if c == 0 else EXTRA)

    @pl.when((col < 4) & (row < 4) & (row >= col))
    def _():
        block = z[pl.ds(pl.multiple_of(jnp.minimum(col, 3) * 256, 256), 256), pl.ds(pl.multiple_of(jnp.minimum(row, 3) * 256, 256), 256)]
        top_ref[:, 0:256] = block.T

    @pl.when((col < 4) & (row < col))
    def _():
        top_ref[:, 0:256] = jnp.zeros((256, 256), F32)

    @pl.when(col < 4)
    def _():
        a = lax.broadcasted_iota(jnp.int32, (1024, 256), 0)
        b = lax.broadcasted_iota(jnp.int32, (1024, 256), 1)
        z[:, 1024:1280] = jnp.where(a == b + col * 256, -1.0, 0.0)

    for k in range(3, -1, -1):
        o, end = 256 * k, 256 * k + 256
        block = inverse_high[k].T, inverse_low[k].T
        side = split(z[o:end, end:1024]) if k < 3 else None
        for c in range(0, 1024, TILE):
            cols = slice(c, c + TILE)
            mine = z[o:end, 1024 + c : 1024 + c + TILE]
            if k < 3:
                mine = mine - product(side, (wh_ref[end:1024, cols], wl_ref[end:1024, cols]))
            wh_ref[o:end, cols], wl_ref[o:end, cols] = split(product(block, split(mine)))

    keep_block.wait()

    @pl.when(col < 4)
    def _():
        m[:, 0:256] = jnp.zeros((2048, 256), F32)

    @pl.loop(PREFIX + 8 * len(HOOKS) + 4 * EXTRA, 16 * (LEAD + COPIES))
    def _(e):
        forward(e, False)

    for s in range(4):
        for t in range(4):
            links = links_of(s, t)
            for d in range(4):

                @pl.when((links // (1 << d)) % 2 == 1)
                def _():
                    block = ar.at[s, pl.ds(t * 512, 512)]
                    remote(block, block, rs.at[s, t, d], rr.at[s, t, 0], around[d]).wait_send()


def panels(matrix):
    sems = [(4, 3), (2, 4), (2, 4), (2, 4), (4, 8, 4), (4, 8), (4, 8), (4, 8), (4, 4, 4), (4, 4, COPIES), (7,)]
    return pl.pallas_call(
        panels_kernel,
        out_shape=[
            jax.ShapeDtypeStruct((2048, 1024), F32),
            jax.ShapeDtypeStruct((4, 2048, 256), F32),
            jax.ShapeDtypeStruct((1024, 1024), BF16),
            jax.ShapeDtypeStruct((1024, 1024), BF16),
            jax.ShapeDtypeStruct((256, 1024), F32),
        ],
        in_specs=[pl.BlockSpec(memory_space=pl.ANY)],
        out_specs=[pl.BlockSpec(memory_space=pltpu.VMEM)] * 5,
        scratch_shapes=[
            pltpu.VMEM((1024, 2048), F32),
            pltpu.VMEM((256, 128), F32),
            pltpu.VMEM((128, 128), F32),
            pltpu.VMEM((4, 256, 256), BF16),
            pltpu.VMEM((4, 256, 256), BF16),
            pltpu.SMEM((16 * (LEAD + COPIES),), jnp.int32),
            *[pltpu.SemaphoreType.DMA(s) for s in sems],
        ],
        compiler_params=pltpu.CompilerParams(collective_id=0, has_side_effects=True, vmem_limit_bytes=26 << 20),
        name="panels",
    )(matrix)


def update_kernel(m, ar, wh, wl, top, out):
    i = pl.program_id(0)
    rows = pl.ds(pl.multiple_of(i * 512, 512), 512)
    total = m[rows]
    left = split(jnp.concatenate([ar[s, rows] for s in range(4)], axis=1))
    out[...] = total - product(left, (wh[...], wl[...]))

    @pl.when((i == 0) & (lax.axis_index("prow") < 4))
    def _():
        out[0:256, :] = top[...]


def shards(matrix):
    return pl.pallas_call(
        update_kernel,
        grid=(4,),
        out_shape=jax.ShapeDtypeStruct((2048, 1024), F32),
        in_specs=[pl.BlockSpec(memory_space=pltpu.VMEM)] * 5,
        out_specs=pl.BlockSpec((512, 1024), lambda i: (i, 0)),
        compiler_params=pltpu.CompilerParams(vmem_limit_bytes=20 << 20),
        name="update",
    )(*panels(matrix))


def solution(mesh):
    return jax.shard_map(
        shards,
        mesh=mesh,
        in_specs=(P("prow", "pcol"),),
        out_specs=P("prow", "pcol"),
        check_vma=False,
    )
```
